256 devices in a mesh: leaf: 64 (over z, x, core), dom: 4 (over y).
Axes of the slice: x: 4, y: 4, z: 8, core: 2. Of those that a mesh axis runs over, the one named last changes fastest.
Arguments:
- child_terms: float32 [1024, 64, 128], P(('leaf', 'dom')), may hold values from -0.5 to 0.5
- transfer: float32 [960, 64, 128], P('leaf')
- top_transfer: float32 [64, 64, 128], replicated
- coupling: float32 [65536, 64, 64], P(('leaf', 'dom')), may hold values from -6 to 6
- block_row: int32 [65536], P(('leaf', 'dom')), may hold values from 0 to 1023, as said below
- block_col: int32 [65536], P(('leaf', 'dom')), may hold values from 0 to 1023, as said below
Outputs:
- bottom_basis: float32 [1024, 64, 128], P(('leaf', 'dom'))
- local_basis: float32 [960, 64, 128], P('leaf')
- top_basis: float32 [64, 64, 128], P('leaf')
- root_factor: float32 [64, 64], replicated
- projected: float32 [65536, 64, 64], P(('leaf', 'dom'))
The draws below stay inside these ranges and needn't reach their ends.
Inputs may be any that keep to these rules, and one draw needn't show every extreme that they name: block_row[b] // 16 == b // 1024. block_col[b] // 16 differs from block_row[b] // 16 by at most 3; both differences -3 and +3 occur.
All inputs are finite; a program needn't handle non-finite values.
Results may differ from the reference program's by a relative error of at most 0.0001.
Values sent between devices are 32-bit elements; how exact they have to be, the bound alone decides.
A program may use at most 128 MiB of HBM per device.

```python
import jax
import jax.numpy as jnp
import numpy as np
from jax import lax

K = 64
NODE_DEV = 16
BLK_DEV = 256
REACH = 3
GROUPS = 64
NODES = 1024
LPAIRS = 960
BLK_LEAF = 1024
BLOCKS = 65536


def pair_draw(key, count, center, spread, off_scale):
    diag_key = jax.random.fold_in(key, 1)
    off_key = jax.random.fold_in(key, 2)
    diag = center + spread * jax.random.uniform(diag_key, (count, 1, 2 * K), jnp.float32, -1.0, 1.0)
    eye = jnp.concatenate([jnp.eye(K, dtype=jnp.float32), jnp.eye(K, dtype=jnp.float32)], axis=1)
    off = off_scale * jax.random.normal(off_key, (count, K, 2 * K), jnp.float32)
    return (eye * diag + off).astype(jnp.float32)


def draw_transfer(key, part):
    key = jax.random.fold_in(key, 11)
    return pair_draw(key, LPAIRS, 0.7, 0.1, 0.15 * K ** (-0.5))


def draw_top_transfer(key, part):
    key = jax.random.fold_in(key, 12)
    return pair_draw(key, GROUPS, 0.7, 0.1, 0.15 * K ** (-0.5))


def draw_block_row(key, part):
    key = jax.random.fold_in(key, 13)
    within = jax.random.randint(key, (BLOCKS,), 0, NODE_DEV, jnp.int32)
    group = jnp.arange(BLOCKS, dtype=jnp.int32) // BLK_LEAF
    return group * NODE_DEV + within


def draw_block_col(key, part):
    key = jax.random.fold_in(key, 14)
    step_key = jax.random.fold_in(key, 1)
    within_key = jax.random.fold_in(key, 2)
    index = jnp.arange(BLOCKS, dtype=jnp.int32)
    group = index // BLK_LEAF
    slot = index % BLK_DEV
    offset = jax.random.randint(step_key, (BLOCKS,), -REACH, REACH + 1, jnp.int32)
    offset = jnp.where(slot == 0, -REACH, jnp.where(slot == 1, REACH, offset))
    target = jnp.clip(group + offset, 0, GROUPS - 1)
    within = jax.random.randint(within_key, (BLOCKS,), 0, NODE_DEV, jnp.int32)
    return target * NODE_DEV + within


def block_scale(key, extent, shards, low, top_value):
    def one(position, shards_of):
        heights = jax.random.uniform(jax.random.fold_in(jax.random.fold_in(key, 6), position), (shards_of,), jnp.float32, low / len(shards), top_value / len(shards))
        return jnp.repeat(jnp.exp(heights), extent[position] // shards_of).reshape((-1,) + (1,) * (len(extent) - position - 1))

    gain = one(*shards[0])
    for cut in shards[1:]:
        gain = gain * one(*cut)
    return gain


def gaussian(own_key, extent, scale, bound, cuts=(), kind=jnp.bfloat16):
    result = scale * jax.random.normal(own_key, extent, jnp.float32)
    if cuts:
        result = result * block_scale(own_key, extent, cuts, -0.22, 0.18)
    return jnp.clip(result, -bound, bound).astype(kind)


def setup_inputs(seed: int = 0) -> dict:
    seeds = jax.random.split(jax.random.key(seed), 7)
    return {
        "child_terms": gaussian(seeds[0], (NODES, K, 2 * K), (2 * K) ** -0.5, 0.5, ((0, 256),), jnp.float32),
        "transfer": draw_transfer(jax.random.fold_in(seeds[6], 71), 0),
        "top_transfer": draw_top_transfer(jax.random.fold_in(seeds[6], 71), 0),
        "coupling": gaussian(seeds[3], (BLOCKS, K, K), 1.0, 6.0, ((0, 256),), jnp.float32),
        "block_row": draw_block_row(jax.random.fold_in(seeds[6], 71), 0),
        "block_col": draw_block_col(jax.random.fold_in(seeds[6], 71), 0),
    }


HIGH = lax.Precision.HIGHEST

def factor(stacked):
    gram = jnp.einsum('nik,njk->nij', stacked, stacked, precision=HIGH)
    lower = jnp.linalg.cholesky(gram)
    basis = jax.vmap(lambda a, b: jax.scipy.linalg.solve_triangular(a, b, lower=True))(lower, stacked)
    return (lower, basis)

def factor_pair(left, right, pair):
    rank = left.shape[-1]
    first = jnp.einsum('nji,njk->nik', pair[:, :, :rank], left, precision=HIGH)
    second = jnp.einsum('nji,njk->nik', pair[:, :, rank:], right, precision=HIGH)
    return factor(jnp.concatenate([first, second], axis=2))

def reference(child_terms, transfer, top_transfer, coupling, block_row, block_col):
    bottom_lower, bottom_basis = factor(child_terms)
    current = bottom_lower.reshape(GROUPS, NODE_DEV, K, K)
    pairs = transfer.reshape(GROUPS, NODE_DEV - 1, K, 2 * K)
    offset = 0
    pieces = []
    while current.shape[1] > 1:
        half = current.shape[1] // 2
        lower, basis = factor_pair(current[:, 0::2].reshape(-1, K, K), current[:, 1::2].reshape(-1, K, K), pairs[:, offset:offset + half].reshape(-1, K, 2 * K))
        current = lower.reshape(GROUPS, half, K, K)
        pieces.append(basis.reshape(GROUPS, half, K, 2 * K))
        offset += half
    local_basis = jnp.concatenate(pieces, axis=1).reshape(LPAIRS, K, 2 * K)
    current = current[:, 0]
    top_basis = jnp.zeros((GROUPS, K, 2 * K), jnp.float32)
    span = 1
    while current.shape[0] > 1:
        count = current.shape[0] // 2
        span = span * 2
        middles = np.arange(count) * span + span // 2
        current, basis = factor_pair(current[0::2], current[1::2], top_transfer[middles])
        top_basis = top_basis.at[middles].set(basis)
    root_factor = jnp.transpose(current[0])
    rows = block_row.reshape(GROUPS, BLK_LEAF)
    cols = block_col.reshape(GROUPS, BLK_LEAF)
    blocks = coupling.reshape(GROUPS, BLK_LEAF, K, K)

    def project(item):
        row_index, col_index, block = item
        half = jnp.einsum('bji,bjk->bik', bottom_lower[row_index], block, precision=HIGH)
        return jnp.einsum('bik,bkl->bil', half, bottom_lower[col_index], precision=HIGH)
    projected = lax.map(project, (rows, cols, blocks)).reshape(BLOCKS, K, K)
    return (bottom_basis, local_basis, top_basis, root_factor, projected)
```

```python
import functools

import jax
import jax.numpy as jnp
from jax import lax
from jax.experimental import pallas as pl
from jax.experimental.pallas import tpu as pltpu
from jax.sharding import PartitionSpec as P

REACH = 3
K = 64
F32 = jnp.float32
BF = jnp.bfloat16
HIGH = lax.Precision.HIGHEST
MESH = pl.DeviceIdType.MESH
NN = ((1,), (0,))
NT = ((1,), (1,))


def dot(a, b, dims):
    return lax.dot_general(a, b, (dims, ((), ())), precision=HIGH, preferred_element_type=F32)


def dot16(a, b):
    return lax.dot_general(a, b, (NN, ((), ())), preferred_element_type=F32)


def split(x):
    high = x.astype(BF)
    return high, (x - high.astype(F32)).astype(BF)


def factor(grams, hook=None):
    count = len(grams)
    sub = lax.broadcasted_iota(jnp.int32, (1, 8, 128), 1)
    row = lax.broadcasted_iota(jnp.int32, (K, K), 0)
    col = lax.broadcasted_iota(jnp.int32, (K, K), 1)
    eye = jnp.where(row == col, 1.0, 0.0).astype(F32)
    rest = jnp.stack([jnp.concatenate([g, eye], axis=1) for g in grams])
    done = []
    for p in range(8):
        panel = rest[:, :8]
        rest = rest[:, 8:]
        left = 56 - 8 * p
        lanes = [8 * p + c for c in range(8)]
        cols = [jnp.broadcast_to(panel[:, :, c : c + 1], (count, 8, 128)) for c in lanes]
        below = [jnp.broadcast_to(rest[:, :, c : c + 1], (count, left, 128)) for c in lanes] if left else []
        out = jnp.zeros((count, 8, 128), F32)
        for k in range(8):
            here = sub == k
            pivot_row = jnp.broadcast_to(panel[:, k : k + 1, :], (count, 8, 128))
            heads = [jnp.broadcast_to(c[:, k : k + 1, :], (count, 8, 128)) for c in cols[k:]]
            out = jnp.where(here, pivot_row * lax.rsqrt(heads[0]), out)
            scale = jnp.where(here, -1.0, cols[k]) * (1.0 / heads[0])
            panel = jnp.where(here, 0.0, panel) - scale * pivot_row
            for c in range(k + 1, 8):
                cols[c] = jnp.where(here, 0.0, cols[c]) - scale * heads[c - k]
        done.append(out)
        for k in range(8 if left else 0):
            rest = rest - below[k] * jnp.broadcast_to(panel[:, k : k + 1, :], (count, left, 128))
        if hook is not None:
            hook(p)
    keep = lax.broadcasted_iota(jnp.int32, (K, 128), 1) >= lax.broadcasted_iota(jnp.int32, (K, 128), 0)
    return [jnp.where(keep, jnp.concatenate([d[n] for d in done], axis=0), 0.0) for n in range(count)]


def kernel(doms, leaves, child, transfer, toptr, coup, rows, cols,
           bottom_out, local_out, top_out, root_out, proj_out,
           win, ct, par, turned, us, lw, rw, xs, xr,
           in_sem, out_sem, gs, gr, ws, wr, bs, br, cs, cr, ds, dr, es, er):
    leaf = lax.axis_index("leaf")
    dom = lax.axis_index("dom")
    top_levels = leaves.bit_length() - 1
    dom_levels = doms.bit_length() - 1
    per = child.shape[0]
    nodes = per * doms
    half = nodes // 2
    last = (2 * REACH + 1) * nodes - 1

    coup_copy = pltpu.make_async_copy(coup, ct, in_sem.at[0])
    coup_copy.start()
    loads = [
        pltpu.make_async_copy(transfer.at[pl.ds(2 * dom, 2)], par.at[pl.ds(0, 2)], in_sem.at[1]),
        pltpu.make_async_copy(transfer.at[pl.ds(half + dom, 1)], par.at[pl.ds(2, 1)], in_sem.at[2]),
        pltpu.make_async_copy(transfer.at[pl.ds(half + doms + dom // 2, 1)], par.at[pl.ds(3, 1)], in_sem.at[3]),
        pltpu.make_async_copy(transfer.at[pl.ds(nodes - 2, 1)], par.at[pl.ds(4, 1)], in_sem.at[4]),
    ]
    for level in range(top_levels):
        step = 2 << level
        middle = leaf // step * step + step // 2
        loads.append(pltpu.make_async_copy(toptr.at[pl.ds(middle, 1)], par.at[pl.ds(5 + level, 1)], in_sem.at[5 + level]))
    for load in loads:
        load.start()

    def near(step):
        return lax.rem(leaf + step + leaves, leaves)

    steps = [s for s in range(-REACH, REACH + 1) if s]
    barrier = pltpu.get_barrier_semaphore()
    for k in range(1, doms):
        pl.semaphore_signal(barrier, inc=1, device_id=(leaf, lax.rem(dom + k, doms)), device_id_type=MESH)
    for s in steps:
        pl.semaphore_signal(barrier, inc=1, device_id=(near(s), dom), device_id_type=MESH)
    for level in range(top_levels):
        other = leaf + (1 - 2 * lax.rem(leaf // (1 << level), 2)) * (1 << level)
        pl.semaphore_signal(barrier, inc=1, device_id=(other, dom), device_id_type=MESH)

    lane = lax.broadcasted_iota(jnp.int32, (K, 128), 1)
    left = lane < K
    side = lane // K

    stacked = [child[n] for n in range(per)]
    current = factor([dot(x, x, NT) for x in stacked])
    for m in range(per // 2):
        tall = jnp.concatenate([current[2 * m][:, :K], current[2 * m + 1][:, :K]], axis=0)
        win[REACH, per // 2 * dom + m] = tall.T
    pl.semaphore_wait(barrier, doms - 1 + len(steps) + top_levels)
    mine = win.at[REACH, pl.ds(per // 2 * dom, per // 2)]
    gather = []
    for k in range(1, doms):
        copy = pltpu.make_async_remote_copy(
            src_ref=mine, dst_ref=mine, send_sem=gs.at[k - 1], recv_sem=gr.at[k - 1],
            device_id=(leaf, lax.rem(dom + k, doms)), device_id_type=MESH)
        copy.start()
        gather.append(copy)
    for n in range(per):
        bottom_out[n] = dot(pltpu.roll(current[n], K, 1)[:, :K], stacked[n], NN)

    for load in loads:
        load.wait()
    for n in range(5 + top_levels):
        pair = par[n]
        par[n] = jnp.concatenate([pair[:, :K], pltpu.roll(pair, K, 1)[:, :K]], axis=0).T

    def product(packed, n):
        wide = jnp.concatenate([jnp.where(left, packed, 0.0), jnp.where(left, 0.0, packed)], axis=0)
        return dot(par[n], wide, NT)

    xa = [product(jnp.where(left, current[2 * s], pltpu.roll(current[2 * s + 1], K, 1)), s) for s in range(per // 2)]
    current = factor([dot(x, x, NT) for x in xa])
    for s in range(per // 2):
        local_out[per // 2 * dom + s] = dot(pltpu.roll(current[s], K, 1)[:, :K], xa[s], NN)
    spread = []
    for k in range(1, doms):
        view = local_out.at[pl.ds(per // 2 * dom, per // 2)]
        copy = pltpu.make_async_remote_copy(
            src_ref=view, dst_ref=view, send_sem=bs.at[k - 1], recv_sem=br.at[k - 1],
            device_id=(leaf, lax.rem(dom + k, doms)), device_id_type=MESH)
        copy.start()
        spread.append(copy)
    x = product(jnp.where(left, current[0], pltpu.roll(current[1], K, 1)), 2)
    (factored,) = factor([dot(x, x, NT)])
    local_out[half + dom] = dot(pltpu.roll(factored, K, 1)[:, :K], x, NN)
    for k in range(1, doms):
        view = local_out.at[pl.ds(half + dom, 1)]
        copy = pltpu.make_async_remote_copy(
            src_ref=view, dst_ref=view, send_sem=cs.at[k - 1], recv_sem=cr.at[k - 1],
            device_id=(leaf, lax.rem(dom + k, doms)), device_id_type=MESH)
        copy.start()
        spread.append(copy)

    for copy in gather:
        copy.wait_recv()
    window = []
    for j, s in enumerate(steps):
        copy = pltpu.make_async_remote_copy(
            src_ref=win.at[REACH], dst_ref=win.at[REACH - s], send_sem=ws.at[j], recv_sem=wr.at[j],
            device_id=(near(s), dom), device_id_type=MESH)
        copy.start()
        window.append(copy)

    def exchange(e, other, bit, factored, hook=None):
        rolled = pltpu.roll(factored, K, 1)
        shaped = jnp.where(bit == 0, factored, rolled)
        xs[e] = shaped
        copy = pltpu.make_async_remote_copy(
            src_ref=xs.at[e], dst_ref=xr.at[e], send_sem=es.at[e], recv_sem=er.at[e],
            device_id=other, device_id_type=MESH)
        copy.start()
        copy.wait_recv()
        x = product(jnp.where(side == bit, shaped, xr[e]), 3 + e)
        (factored,) = factor([dot(x, x, NT)], hook)
        return factored, dot(pltpu.roll(factored, K, 1)[:, :K], x, NN)

    bit = lax.rem(dom, 2)
    factored, basis = exchange(0, (leaf, dom + 1 - 2 * bit), bit, factored)
    place = half + doms + dom // 2
    local_out[place] = basis
    view = local_out.at[pl.ds(place, 1)]
    copy = pltpu.make_async_remote_copy(
        src_ref=view, dst_ref=view, send_sem=ds, recv_sem=dr,
        device_id=(leaf, lax.rem(dom + 2, doms)), device_id_type=MESH)
    copy.start()
    spread.append(copy)
    bit = dom // 2
    factored, basis = exchange(1, (leaf, dom + (1 - 2 * bit) * 2), bit, factored)
    local_out[nodes - 2] = basis

    top_out[0] = jnp.zeros((K, 128), F32)

    def climb(level, factored):
        step = jnp.int32(1)
        for r in range(1, top_levels):
            step = jnp.where(level == r, 1 << r, step)
        bit = lax.rem(leaf // step, 2)
        factored, basis = exchange(dom_levels + level, (leaf + (1 - 2 * bit) * step, dom), bit, factored)
        middle = leaf // (2 * step) * (2 * step) + step
        top_out[0] = jnp.where(middle == leaf, basis, top_out[0])
        return factored

    factored = lax.fori_loop(0, top_levels, climb, factored)
    root_out[...] = factored[:, :K]

    coup_copy.wait()

    def turn(i, carry):
        slab = jnp.concatenate([ct[i, :, 0:128], ct[i, :, 128:256]], axis=0)
        turned[pl.ds(i, 128, K), :] = slab.T
        return carry

    lax.fori_loop(0, K, turn, 0, unroll=4)

    def expand_rows(m, carry):
        pair = win[REACH, m]
        both = jnp.concatenate([pair, pair], axis=0).T
        high = both.astype(BF)
        low = jnp.where(lax.broadcasted_iota(jnp.int32, (128, 128), 1) < K, both - high.astype(F32), 0.0).astype(BF)
        for h in range(2):
            us[2 * m + h, :, 0:128] = high[K * h : K * h + K]
            us[2 * m + h, :, 128:256] = low[K * h : K * h + K]
        return carry

    lax.fori_loop(0, half, expand_rows, 0, unroll=2)

    def row_side(b, carry):
        off = pl.multiple_of(b * K, K)
        high, low = split(turned[pl.ds(off, K), :])
        weights = jnp.concatenate([high, low, high, jnp.zeros_like(high)], axis=0)
        first = lax.rem(rows[b], nodes)
        second = lax.rem(rows[b + 128], nodes)
        both = dot16(jnp.concatenate([us[first], us[second]], axis=0), weights)
        turned[pl.ds(off, K), :] = jnp.where(left, both[:K], both[K:])
        return carry

    lax.fori_loop(0, 128, row_side, 0, unroll=8)

    for copy in window:
        copy.wait_recv()

    def expand_cols(q, carry):
        s = q // half
        m = q % half
        pair = win[s, m]
        rolled = pltpu.roll(pair, K, 1)
        for h, (a, b) in enumerate(((pair, rolled), (rolled, pair))):
            for ref, value in ((lw, jnp.where(left, a, 0.0)), (rw, jnp.where(left, 0.0, b))):
                high, low = split(value)
                ref[2 * q + h, :, 0:128] = high
                ref[2 * q + h, :, 128:256] = low
        return carry

    lax.fori_loop(0, (2 * REACH + 1) * half, expand_cols, 0, unroll=4)

    def col_side(b, carry):
        off = pl.multiple_of(b * K, K)
        high, low = split(turned[pl.ds(off, K), :])
        first = jnp.clip(cols[b] - (leaf - REACH) * nodes, 0, last)
        second = jnp.clip(cols[b + 128] - (leaf - REACH) * nodes, 0, last)
        weights = jnp.concatenate([lw[first], rw[second]], axis=0)
        both = dot16(jnp.concatenate([high, low], axis=0), weights)
        turned[pl.ds(off, K), :] = both[:K, :128] + both[K:, :128] + both[:K, 128:]
        return carry

    lax.fori_loop(0, 128, col_side, 0, unroll=8)

    def turn_back(i, carry):
        slab = turned[pl.ds(i, 128, K), :].T
        ct[i, :, 0:128] = slab[:K]
        ct[i, :, 128:256] = slab[K:]
        return carry

    parts = 4
    stores = []
    for part in range(parts):
        lax.fori_loop(K // parts * part, K // parts * (part + 1), turn_back, 0, unroll=4)
        span = pl.ds(K // parts * part, K // parts)
        copy = pltpu.make_async_copy(ct.at[span], proj_out.at[span], out_sem.at[part])
        copy.start()
        stores.append(copy)
    for copy in stores:
        copy.wait()

    for copy in spread:
        copy.wait_recv()
    for copy in gather + spread + window:
        copy.wait_send()

    def drain(e, carry):
        pltpu.make_async_remote_copy(
            src_ref=xs.at[e], dst_ref=xr.at[e], send_sem=es.at[e], recv_sem=er.at[e],
            device_id=(leaf, dom), device_id_type=MESH).wait_send()
        return carry

    lax.fori_loop(0, dom_levels + top_levels, drain, 0)


def on_device(doms, leaves, child_terms, transfer, top_transfer, coupling, block_row, block_col):
    per = child_terms.shape[0]
    nodes = per * doms
    top_levels = leaves.bit_length() - 1
    exchanges = top_levels + doms.bit_length() - 1
    vmem = pl.BlockSpec(memory_space=pltpu.VMEM)
    smem = pl.BlockSpec(memory_space=pltpu.SMEM)
    hbm = pl.BlockSpec(memory_space=pl.ANY)
    dma = pltpu.SemaphoreType.DMA
    sides = 2 * REACH
    bottom, local, top, root, projected = pl.pallas_call(
        functools.partial(kernel, doms, leaves),
        out_shape=(
            jax.ShapeDtypeStruct((per, K, 2 * K), F32),
            jax.ShapeDtypeStruct((nodes - 1, K, 2 * K), F32),
            jax.ShapeDtypeStruct((1, K, 2 * K), F32),
            jax.ShapeDtypeStruct((K, K), F32),
            jax.ShapeDtypeStruct((K, K, 256), F32),
        ),
        in_specs=[vmem, hbm, hbm, hbm, smem, smem],
        out_specs=(vmem, vmem, vmem, vmem, hbm),
        scratch_shapes=[
            pltpu.VMEM((sides + 1, nodes // 2, K, 128), F32),
            pltpu.VMEM((K, K, 256), F32),
            pltpu.VMEM((5 + top_levels, K, 128), F32),
            pltpu.VMEM((128 * K, 128), F32),
            pltpu.VMEM((nodes, K, 256), BF),
            pltpu.VMEM(((sides + 1) * nodes, K, 256), BF),
            pltpu.VMEM(((sides + 1) * nodes, K, 256), BF),
            pltpu.VMEM((exchanges, K, 128), F32),
            pltpu.VMEM((exchanges, K, 128), F32),
            dma((5 + top_levels,)),
            dma((4,)),
            dma((doms - 1,)), dma((doms - 1,)),
            dma((sides,)), dma((sides,)),
            dma((doms - 1,)), dma((doms - 1,)),
            dma((doms - 1,)), dma((doms - 1,)),
            dma, dma,
            dma((exchanges,)), dma((exchanges,)),
        ],
        compiler_params=pltpu.CompilerParams(
            collective_id=0, has_side_effects=True, vmem_limit_bytes=48 * 2**20),
    )(child_terms, transfer, top_transfer, jnp.transpose(coupling, (1, 2, 0)), block_row, block_col)
    return bottom, local, top, root, jnp.transpose(projected, (2, 0, 1))


def solution(mesh):
    split_all = P(("leaf", "dom"), None, None)
    placed = (split_all, P("leaf", None, None), P(), split_all, P(("leaf", "dom")), P(("leaf", "dom")))
    return jax.shard_map(
        functools.partial(on_device, mesh.shape["dom"], mesh.shape["leaf"]),
        mesh=mesh,
        in_specs=placed,
        out_specs=(split_all, P("leaf", None, None), P("leaf", None, None), P(), split_all),
        check_vma=False,
    )
```

```python
import functools
import itertools

import jax
import jax.numpy as jnp
from jax import lax
from jax.experimental import pallas as pl
from jax.experimental.pallas import tpu as pltpu
from jax.sharding import PartitionSpec as P

REACH = 3
K = 64
F32 = jnp.float32
BF = jnp.bfloat16
HIGH = lax.Precision.HIGHEST
MESH = pl.DeviceIdType.MESH
NN = ((1,), (0,))
NT = ((1,), (1,))


def dot(a, b, dims):
    return lax.dot_general(a, b, (dims, ((), ())), precision=HIGH, preferred_element_type=F32)


def dot16(a, b):
    return lax.dot_general(a, b, (NN, ((), ())), preferred_element_type=F32)


def split(x):
    high = x.astype(BF)
    return high, (x - high.astype(F32)).astype(BF)


def factor(grams, hook=None):
    count = len(grams)
    sub = lax.broadcasted_iota(jnp.int32, (1, 8, 128), 1)
    row = lax.broadcasted_iota(jnp.int32, (K, K), 0)
    col = lax.broadcasted_iota(jnp.int32, (K, K), 1)
    eye = jnp.where(row == col, 1.0, 0.0).astype(F32)
    rest = jnp.stack([jnp.concatenate([g, eye], axis=1) for g in grams])
    done = []
    for p in range(8):
        panel = rest[:, :8]
        rest = rest[:, 8:]
        left = 56 - 8 * p
        lanes = [8 * p + c for c in range(8)]
        cols = [jnp.broadcast_to(panel[:, :, c : c + 1], (count, 8, 128)) for c in lanes]
        below = [jnp.broadcast_to(rest[:, :, c : c + 1], (count, left, 128)) for c in lanes] if left else []
        out = jnp.zeros((count, 8, 128), F32)
        for k in range(8):
            here = sub == k
            pivot_row = jnp.broadcast_to(panel[:, k : k + 1, :], (count, 8, 128))
            heads = [jnp.broadcast_to(c[:, k : k + 1, :], (count, 8, 128)) for c in cols[k:]]
            out = jnp.where(here, pivot_row * lax.rsqrt(heads[0]), out)
            scale = jnp.where(here, -1.0, cols[k]) * (1.0 / heads[0])
            panel = jnp.where(here, 0.0, panel) - scale * pivot_row
            for c in range(k + 1, 8):
                cols[c] = jnp.where(here, 0.0, cols[c]) - scale * heads[c - k]
        done.append(out)
        for k in range(8 if left else 0):
            rest = rest - below[k] * jnp.broadcast_to(panel[:, k : k + 1, :], (count, left, 128))
        if hook is not None:
            hook(p)
    keep = lax.broadcasted_iota(jnp.int32, (K, 128), 1) >= lax.broadcasted_iota(jnp.int32, (K, 128), 0)
    return [jnp.where(keep, jnp.concatenate([d[n] for d in done], axis=0), 0.0) for n in range(count)]


def kernel(doms, leaves, child_hbm, transfer, toptr, coup, rows_hbm, cols_hbm,
           bottom_hbm, local_hbm, top_hbm, root_hbm, turned_hbm,
           bottom_out, local_out, top_out, root_out, turned,
           child, rows, cols, win, ct, par, us, lw, rw, xr,
           in_sem, out_sem, gs, gr, ws, wr, bs, br, cs, cr, es, er):
    leaf = lax.axis_index("leaf")
    dom = lax.axis_index("dom")
    top_levels = leaves.bit_length() - 1
    dom_levels = doms.bit_length() - 1
    stages = (top_levels + dom_levels) // 2
    per = child.shape[0]
    nodes = per * doms
    half = nodes // 2
    own = per // 2
    last = (2 * REACH + 1) * nodes - 1

    child_copy = pltpu.make_async_copy(child_hbm, child, in_sem.at[0])
    child_copy.start()
    loads = [
        pltpu.make_async_copy(transfer.at[pl.ds(own * dom, own)], par.at[pl.ds(0, own)], in_sem.at[1]),
        pltpu.make_async_copy(transfer.at[pl.ds(half + dom, 1)], par.at[pl.ds(2, 1)], in_sem.at[2]),
        pltpu.make_async_copy(transfer.at[pl.ds(half + doms, 3)], par.at[pl.ds(3, 3)], in_sem.at[3]),
    ]
    bases = []
    for t in range(stages - 1):
        step = 4**t
        base = leaf // (4 * step) * (4 * step)
        bases.append([base + step * r for r in (1, 3, 2)])
        for r in range(3):
            n = 3 * (t + 2) + r
            loads.append(pltpu.make_async_copy(toptr.at[pl.ds(bases[t][r], 1)], par.at[pl.ds(n, 1)], in_sem.at[n - 2]))
    for load in loads:
        load.start()
    index_loads = [
        pltpu.make_async_copy(rows_hbm, rows, in_sem.at[3 * stages + 1]),
        pltpu.make_async_copy(cols_hbm, cols, in_sem.at[3 * stages + 2]),
    ]
    for load in index_loads:
        load.start()
    coup_copy = pltpu.make_async_copy(coup, ct, in_sem.at[3 * stages + 3])
    coup_copy.start()

    def near(step):
        return lax.rem(leaf + step + leaves, leaves)

    def dom_peer(step):
        return (leaf, lax.rem(dom + step, doms))

    steps = [s for s in range(-REACH, REACH + 1) if s]
    groups = [(dom, [dom_peer(k) for k in range(1, 4)])]
    for t in range(stages - 1):
        step = 4**t
        spot = lax.rem(leaf // step, 4)
        groups.append((spot, [(leaf + (lax.rem(spot + k, 4) - spot) * step, dom) for k in range(1, 4)]))
    greeted = [(near(s), dom) for s in steps]
    for _, others in groups:
        greeted += others
    barrier = pltpu.get_barrier_semaphore()
    for other in greeted:
        pl.semaphore_signal(barrier, inc=1, device_id=other, device_id_type=MESH)

    lane = lax.broadcasted_iota(jnp.int32, (K, 128), 1)
    left = lane < K
    started = []

    def send(src, dst, send_sem, recv_sem, other):
        copy = pltpu.make_async_remote_copy(
            src_ref=src, dst_ref=dst, send_sem=send_sem, recv_sem=recv_sem,
            device_id=other, device_id_type=MESH)
        copy.start()
        started.append(copy)
        return copy

    def spread(view, send_sems, recv_sems):
        return [send(view, view, send_sems.at[k - 1], recv_sems.at[k - 1], dom_peer(k)) for k in range(1, doms)]

    def inverse(factored):
        return pltpu.roll(factored, K, 1)[:, :K]

    def turn(i, carry):
        slab = jnp.concatenate([ct[i, :, 0:128], ct[i, :, 128:256]], axis=0)
        turned[pl.ds(i, 128, K), :] = slab.T
        return carry

    def expand_rows(m, carry):
        pair = win[REACH, m]
        both = jnp.concatenate([pair, pair], axis=0).T
        high = both.astype(BF)
        low = jnp.where(lax.broadcasted_iota(jnp.int32, (128, 128), 1) < K, both - high.astype(F32), 0.0).astype(BF)
        for h in range(2):
            us[2 * m + h, :, 0:128] = high[K * h : K * h + K]
            us[2 * m + h, :, 128:256] = low[K * h : K * h + K]
        return carry

    def row_side(b, carry):
        off = pl.multiple_of(b * K, K)
        high, low = split(turned[pl.ds(off, K), :])
        weights = jnp.concatenate([high, low, high, jnp.zeros_like(high)], axis=0)
        first = lax.rem(rows[b], nodes)
        second = lax.rem(rows[b + 128], nodes)
        both = dot16(jnp.concatenate([us[first], us[second]], axis=0), weights)
        turned[pl.ds(off, K), :] = jnp.where(left, both[:K], both[K:])
        return carry

    def expand_cols(q, carry):
        s = q // half
        m = q % half
        pair = win[s, m]
        rolled = pltpu.roll(pair, K, 1)
        for h, (a, b) in enumerate(((pair, rolled), (rolled, pair))):
            for ref, value in ((lw, jnp.where(left, a, 0.0)), (rw, jnp.where(left, 0.0, b))):
                high, low = split(value)
                ref[2 * q + h, :, 0:128] = high
                ref[2 * q + h, :, 128:256] = low
        return carry

    def col_side(b, carry):
        off = pl.multiple_of(b * K, K)
        high, low = split(turned[pl.ds(off, K), :])
        first = jnp.clip(cols[b] - (leaf - REACH) * nodes, 0, last)
        second = jnp.clip(cols[b + 128] - (leaf - REACH) * nodes, 0, last)
        weights = jnp.concatenate([lw[first], rw[second]], axis=0)
        both = dot16(jnp.concatenate([high, low], axis=0), weights)
        turned[pl.ds(off, K), :] = both[:K, :128] + both[K:, :128] + both[:K, 128:]
        return carry

    def run(body, first, past, unroll):
        lax.fori_loop(first, past, body, 0, unroll=unroll)

    pairs = (2 * REACH + 1) * half
    window = []

    def prepare():
        for load in index_loads:
            load.wait()
        for arrival in gather:
            arrival.wait_recv()
        for j, s in enumerate(steps):
            window.append(send(win.at[REACH], win.at[REACH - s], ws.at[j], wr.at[j], (near(s), dom)))
        run(expand_rows, 0, half, 2)

    def widen():
        for copy in window:
            copy.wait_recv()
        run(expand_cols, 0, pairs, 4)

    queues = {"turn": iter(range(K)), "row": iter(range(128)), "col": iter(range(128))}
    bodies = {"turn": turn, "row": row_side, "col": col_side}

    def hook(kind, count):
        def emit(_):
            for _ in range(count):
                n = next(queues[kind], None)
                if n is not None:
                    bodies[kind](n, 0)
        return emit

    def chunk(kind, count, unroll):
        taken = list(itertools.islice(queues[kind], count))
        run(bodies[kind], taken[0], taken[-1] + 1, unroll)

    def fill(stage):
        if stage == 0:
            chunk("turn", 32, 4)
            prepare()
        elif stage == stages - 3:
            chunk("row", 48, 8)
        elif stage == stages - 2:
            chunk("row", None, 8)
            widen()
        elif stage == stages - 1:
            chunk("col", 48, 8)

    hooks = {0: ("row", 2, 2), stages - 3: ("row", 2, 2), stages - 2: ("col", 2, 2), stages - 1: ("col", 6, 0)}

    child_copy.wait()
    stacked = [child[n] for n in range(per)]
    current = factor([dot(x, x, NT) for x in stacked])
    for m in range(own):
        tall = jnp.concatenate([current[2 * m][:, :K], current[2 * m + 1][:, :K]], axis=0)
        win[REACH, own * dom + m] = tall.T
    pl.semaphore_wait(barrier, len(greeted))
    mine = win.at[REACH, pl.ds(own * dom, own)]
    gather = spread(mine, gs, gr)

    for load in loads:
        load.wait()
    for n in range(3 * stages + 3):
        pair = par[n]
        par[n] = jnp.concatenate([pair[:, :K], pltpu.roll(pair, K, 1)[:, :K]], axis=0).T

    def product(packed, n):
        wide = jnp.concatenate([jnp.where(left, packed, 0.0), jnp.where(left, 0.0, packed)], axis=0)
        return dot(par[n], wide, NT)

    xa = [product(jnp.where(left, current[2 * s], pltpu.roll(current[2 * s + 1], K, 1)), s) for s in range(own)]
    below = current
    coup_copy.wait()
    current = factor([dot(x, x, NT) for x in xa], hook("turn", 2))
    x = product(jnp.where(left, current[0], pltpu.roll(current[1], K, 1)), own)
    for n in range(per):
        bottom_out[n] = dot(inverse(below[n]), stacked[n], NN)
    stores = [pltpu.make_async_copy(bottom_out, bottom_hbm, out_sem.at[0])]
    stores[0].start()
    for s in range(own):
        local_out[own * dom + s] = dot(inverse(current[s]), xa[s], NN)
    arrivals = spread(local_out.at[pl.ds(own * dom, own)], bs, br)
    (factored,) = factor([dot(x, x, NT)], hook("turn", 2))

    top_out[0] = jnp.zeros((K, 128), F32)

    def keep_bases(stage, lowers, xs, top, x):
        if stage == 0:
            for r, (lower, value) in enumerate(zip(lowers + [top], xs + [x])):
                local_out[half + doms + r] = dot(inverse(lower), value, NN)
            return
        first, second, middle = bases[stage - 1]
        at_first, at_middle = first == leaf, middle == leaf
        lower = jnp.where(at_middle, top, jnp.where(at_first, lowers[0], lowers[1]))
        value = jnp.where(at_middle, x, jnp.where(at_first, xs[0], xs[1]))
        found = at_first | at_middle | (second == leaf)
        top_out[0] = jnp.where(found, dot(inverse(lower), value, NN), top_out[0])

    pending = None
    for stage in range(stages):
        spot, others = groups[stage]
        xr[stage, spot] = jnp.where(lax.rem(spot, 2) == 0, factored, pltpu.roll(factored, K, 1))
        view = xr.at[stage, spot]
        copies = [send(view, view, es.at[stage, k], er.at[stage, k], others[k]) for k in range(3)]
        if stage == 0:
            local_out[half + dom] = dot(inverse(factored), x, NN)
            arrivals += spread(local_out.at[pl.ds(half + dom, 1)], cs, cr)
        else:
            keep_bases(*pending)
        fill(stage)
        for copy in copies:
            copy.wait_recv()
        kind, low, high = hooks.get(stage, ("row", 0, 0))
        xs = [product(jnp.where(left, xr[stage, 2 * s], xr[stage, 2 * s + 1]), 3 * stage + 3 + s) for s in range(2)]
        lowers = factor([dot(v, v, NT) for v in xs], hook(kind, low))
        if stage == stages - 1:
            stores.append(pltpu.make_async_copy(turned, turned_hbm, out_sem.at[1]))
            stores[-1].start()
            for copy in arrivals:
                copy.wait_recv()
            stores.append(pltpu.make_async_copy(local_out, local_hbm, out_sem.at[2]))
            stores[-1].start()
        x = product(jnp.where(left, lowers[0], pltpu.roll(lowers[1], K, 1)), 3 * stage + 5)
        (factored,) = factor([dot(x, x, NT)], hook(kind, high))
        pending = (stage, lowers, xs, factored, x)
    root_out[...] = factored[:, :K]
    stores.append(pltpu.make_async_copy(root_out, root_hbm, out_sem.at[3]))
    stores[-1].start()
    keep_bases(*pending)
    stores.append(pltpu.make_async_copy(top_out, top_hbm, out_sem.at[4]))
    stores[-1].start()

    for copy in started:
        copy.wait_send()
    for copy in stores:
        copy.wait()


def finish(bottom, local, top, root, turned, bottom_out, local_out, top_out, root_out, proj_out,
           bottom_in, local_in, top_in, root_in, parts_in, ct, load_sem, part_sem, store_sem, out_sem):
    parts, _, deep, _ = parts_in.shape
    part_loads = []
    for part in range(parts):
        copy = pltpu.make_async_copy(turned.at[:, pl.ds(deep * part, deep)], parts_in.at[part], part_sem.at[part])
        copy.start()
        part_loads.append(copy)
    small = ((bottom, bottom_in, bottom_out), (local, local_in, local_out), (top, top_in, top_out), (root, root_in, root_out))
    loads = [pltpu.make_async_copy(src, mid, load_sem.at[n]) for n, (src, mid, _) in enumerate(small)]
    stores = [pltpu.make_async_copy(mid, dst, store_sem.at[n]) for n, (_, mid, dst) in enumerate(small)]
    for load in loads:
        load.start()
    for part in range(parts):
        part_loads[part].wait()
        for r in range(deep):
            slab = parts_in[part, :, r, :].T
            ct[deep * part + r, :, 0:128] = slab[:K]
            ct[deep * part + r, :, 128:256] = slab[K:]
        span = pl.ds(deep * part, deep)
        copy = pltpu.make_async_copy(ct.at[span], proj_out.at[span], out_sem.at[part])
        copy.start()
        stores.append(copy)
        if part == 0:
            for load, store in zip(loads, stores):
                load.wait()
                store.start()
    for copy in stores:
        copy.wait()


def on_device(doms, leaves, child_terms, transfer, top_transfer, coupling, block_row, block_col):
    per = child_terms.shape[0]
    nodes = per * doms
    top_levels = leaves.bit_length() - 1
    stages = (top_levels + doms.bit_length() - 1) // 2
    hbm = pl.BlockSpec(memory_space=pltpu.HBM)
    dma = pltpu.SemaphoreType.DMA
    sides = 2 * REACH
    small_shapes = ((per, K, 2 * K), (nodes - 1, K, 2 * K), (1, K, 2 * K), (K, K))
    small = tuple(jax.ShapeDtypeStruct(shape, F32) for shape in small_shapes)
    small_scratch = [pltpu.VMEM(shape, F32) for shape in small_shapes]
    *ready, turned = pl.pallas_call(
        functools.partial(kernel, doms, leaves),
        out_shape=small + (jax.ShapeDtypeStruct((128 * K, 128), F32),),
        in_specs=[hbm] * 6,
        out_specs=(hbm,) * 5,
        scratch_shapes=small_scratch + [
            pltpu.VMEM((128 * K, 128), F32),
            pltpu.VMEM((per, K, 128), F32),
            pltpu.SMEM((256,), jnp.int32),
            pltpu.SMEM((256,), jnp.int32),
            pltpu.VMEM((sides + 1, nodes // 2, K, 128), F32),
            pltpu.VMEM((K, K, 256), F32),
            pltpu.VMEM((3 * stages + 3, K, 128), F32),
            pltpu.VMEM((nodes, K, 256), BF),
            pltpu.VMEM(((sides + 1) * nodes, K, 256), BF),
            pltpu.VMEM(((sides + 1) * nodes, K, 256), BF),
            pltpu.VMEM((stages, 4, K, 128), F32),
            dma((3 * stages + 4,)),
            dma((5,)),
            dma((doms - 1,)), dma((doms - 1,)),
            dma((sides,)), dma((sides,)),
            dma((doms - 1,)), dma((doms - 1,)),
            dma((doms - 1,)), dma((doms - 1,)),
            dma((stages, 3)), dma((stages, 3)),
        ],
        compiler_params=pltpu.CompilerParams(
            collective_id=0, has_side_effects=True, vmem_limit_bytes=60 * 2**20),
    )(child_terms, transfer, top_transfer, jnp.transpose(coupling, (1, 2, 0)), block_row, block_col)
    bottom, local, top, root, projected = pl.pallas_call(
        finish,
        out_shape=small + (jax.ShapeDtypeStruct((K, K, 256), F32),),
        in_specs=[hbm] * 5,
        out_specs=(hbm,) * 5,
        scratch_shapes=small_scratch + [
            pltpu.VMEM((4, 128, K // 4, 128), F32), pltpu.VMEM((K, K, 256), F32),
            dma((4,)), dma((4,)), dma((4,)), dma((4,)),
        ],
        compiler_params=pltpu.CompilerParams(vmem_limit_bytes=60 * 2**20),
    )(*ready, turned.reshape(128, K, 128))
    return bottom, local, top, root, jnp.transpose(projected, (2, 0, 1))


def solution(mesh):
    split_all = P(("leaf", "dom"), None, None)
    placed = (split_all, P("leaf", None, None), P(), split_all, P(("leaf", "dom")), P(("leaf", "dom")))
    return jax.shard_map(
        functools.partial(on_device, mesh.shape["dom"], mesh.shape["leaf"]),
        mesh=mesh,
        in_specs=placed,
        out_specs=(split_all, P("leaf", None, None), P("leaf", None, None), P(), split_all),
        check_vma=False,
    )
```

```python
import functools
import itertools

import jax
import jax.numpy as jnp
from jax import lax
from jax.experimental import pallas as pl
from jax.experimental.pallas import tpu as pltpu
from jax.sharding import PartitionSpec as P

REACH = 3
K = 64
F32 = jnp.float32
BF = jnp.bfloat16
HIGH = lax.Precision.HIGHEST
MESH = pl.DeviceIdType.MESH
NN = ((1,), (0,))
NT = ((1,), (1,))


def dot(a, b, dims):
    return lax.dot_general(a, b, (dims, ((), ())), precision=HIGH, preferred_element_type=F32)


def dot16(a, b):
    return lax.dot_general(a, b, (NN, ((), ())), preferred_element_type=F32)


def split(x):
    high = x.astype(BF)
    return high, (x - high.astype(F32)).astype(BF)


WIDE = 16
TURN_FILL = 32
ROW_FILL = 48
ROW_HOOK = 16
COL_FILL = 48
COL_HOOK = 48


def factor(grams, hook=None):
    full = (WIDE, 128)
    sub = lax.broadcasted_iota(jnp.int32, full, 0)
    row = lax.broadcasted_iota(jnp.int32, (K, K), 0)
    col = lax.broadcasted_iota(jnp.int32, (K, K), 1)
    eye = jnp.where(row == col, 1.0, 0.0).astype(F32)
    rests = [jnp.concatenate([g, eye], axis=1) for g in grams]
    dones = [[] for _ in grams]

    def spread_row(value, k):
        return jnp.broadcast_to(value[k : k + 1, :], full)

    for p in range(K // WIDE):
        states = []
        for rest in rests:
            panel = rest[:WIDE]
            cols = [jnp.broadcast_to(panel[:, c : c + 1], full) for c in range(WIDE * p, WIDE * p + WIDE)]
            states.append([panel, cols, jnp.zeros(full, F32)])
        for k in range(0, WIDE, 2):
            here, below = sub == k, sub == k + 1
            both = here | below
            for state in states:
                panel, cols, out = state
                row0, row1 = spread_row(panel, k), spread_row(panel, k + 1)
                tops = [spread_row(c, k) for c in cols[k:]]
                nexts = [spread_row(c, k + 1) for c in cols[k:]]
                inv0 = 1.0 / tops[0]
                down, right = nexts[0] * inv0, tops[1] * inv0
                pivot1 = nexts[1] - down * tops[1]
                inv1 = 1.0 / pivot1
                first = jnp.where(here, -1.0, jnp.where(below, 0.0, cols[k]))
                second = jnp.where(below, -1.0, jnp.where(here, 0.0, cols[k + 1]))
                scale0 = first * inv0
                scale1 = (second - right * first) * inv1
                reduced = row1 - down * row0
                state[2] = jnp.where(here, row0 * lax.rsqrt(tops[0]), jnp.where(below, reduced * lax.rsqrt(pivot1), out))
                state[0] = (jnp.where(both, 0.0, panel) - scale0 * row0) - scale1 * reduced
                for c in range(k + 2, WIDE):
                    rest_col = nexts[c - k] - down * tops[c - k]
                    cols[c] = (jnp.where(both, 0.0, cols[c]) - scale0 * tops[c - k]) - scale1 * rest_col
            if hook is not None:
                hook((p * WIDE + k) // 2)
        for n, (panel, _, out) in enumerate(states):
            dones[n].append(out)
            tail = rests[n][WIDE:]
            height = tail.shape[0]
            if height:
                terms = [
                    jnp.broadcast_to(tail[:, c : c + 1], (height, 128)) * jnp.broadcast_to(panel[k : k + 1, :], (height, 128))
                    for k, c in enumerate(range(WIDE * p, WIDE * p + WIDE))
                ]
                while len(terms) > 1:
                    terms = [x + y for x, y in zip(terms[0::2], terms[1::2])]
                rests[n] = tail - terms[0]
    keep = lax.broadcasted_iota(jnp.int32, (K, 128), 1) >= lax.broadcasted_iota(jnp.int32, (K, 128), 0)
    return [jnp.where(keep, jnp.concatenate(done, axis=0), 0.0) for done in dones]


def kernel(doms, leaves, child_hbm, transfer, toptr, coup, rows_hbm, cols_hbm,
           bottom_hbm, local_hbm, top_hbm, root_hbm, turned_hbm,
           bottom_out, local_out, top_out, root_out, turned,
           child, rows, cols, win, ct, par, us, lw, rw, xr,
           in_sem, out_sem, gs, gr, ws, wr, bs, br, cs, cr, es, er):
    leaf = lax.axis_index("leaf")
    dom = lax.axis_index("dom")
    top_levels = leaves.bit_length() - 1
    dom_levels = doms.bit_length() - 1
    stages = (top_levels + dom_levels) // 2
    per = child.shape[0]
    nodes = per * doms
    half = nodes // 2
    own = per // 2
    last = (2 * REACH + 1) * nodes - 1

    child_copy = pltpu.make_async_copy(child_hbm, child, in_sem.at[0])
    child_copy.start()
    loads = [
        pltpu.make_async_copy(transfer.at[pl.ds(own * dom, own)], par.at[pl.ds(0, own)], in_sem.at[1]),
        pltpu.make_async_copy(transfer.at[pl.ds(half + dom, 1)], par.at[pl.ds(2, 1)], in_sem.at[2]),
        pltpu.make_async_copy(transfer.at[pl.ds(half + doms, 3)], par.at[pl.ds(3, 3)], in_sem.at[3]),
    ]
    bases = []
    for t in range(stages - 1):
        step = 4**t
        base = leaf // (4 * step) * (4 * step)
        bases.append([base + step * r for r in (1, 3, 2)])
        for r in range(3):
            n = 3 * (t + 2) + r
            loads.append(pltpu.make_async_copy(toptr.at[pl.ds(bases[t][r], 1)], par.at[pl.ds(n, 1)], in_sem.at[n - 2]))
    for load in loads:
        load.start()
    index_loads = [
        pltpu.make_async_copy(rows_hbm, rows, in_sem.at[3 * stages + 1]),
        pltpu.make_async_copy(cols_hbm, cols, in_sem.at[3 * stages + 2]),
    ]
    for load in index_loads:
        load.start()
    coup_copy = pltpu.make_async_copy(coup, ct, in_sem.at[3 * stages + 3])
    coup_copy.start()

    def near(step):
        return lax.rem(leaf + step + leaves, leaves)

    def dom_peer(step):
        return (leaf, lax.rem(dom + step, doms))

    steps = [s for s in range(-REACH, REACH + 1) if s]
    groups = [(dom, [dom_peer(k) for k in range(1, 4)])]
    for t in range(stages - 1):
        step = 4**t
        spot = lax.rem(leaf // step, 4)
        groups.append((spot, [(leaf + (lax.rem(spot + k, 4) - spot) * step, dom) for k in range(1, 4)]))
    greeted = [(near(s), dom) for s in steps]
    for _, others in groups:
        greeted += others
    barrier = pltpu.get_barrier_semaphore()
    for other in greeted:
        pl.semaphore_signal(barrier, inc=1, device_id=other, device_id_type=MESH)

    lane = lax.broadcasted_iota(jnp.int32, (K, 128), 1)
    left = lane < K
    started = []

    def send(src, dst, send_sem, recv_sem, other):
        copy = pltpu.make_async_remote_copy(
            src_ref=src, dst_ref=dst, send_sem=send_sem, recv_sem=recv_sem,
            device_id=other, device_id_type=MESH)
        copy.start()
        started.append(copy)
        return copy

    def spread(view, send_sems, recv_sems):
        return [send(view, view, send_sems.at[k - 1], recv_sems.at[k - 1], dom_peer(k)) for k in range(1, doms)]

    def inverse(factored):
        return pltpu.roll(factored, K, 1)[:, :K]

    def turn(i, carry):
        slab = jnp.concatenate([ct[i, :, 0:128], ct[i, :, 128:256]], axis=0)
        turned[pl.ds(i, 128, K), :] = slab.T
        return carry

    def expand_rows(m, carry):
        pair = win[REACH, m]
        both = jnp.concatenate([pair, pair], axis=0).T
        high = both.astype(BF)
        low = jnp.where(lax.broadcasted_iota(jnp.int32, (128, 128), 1) < K, both - high.astype(F32), 0.0).astype(BF)
        for h in range(2):
            us[2 * m + h, :, 0:128] = high[K * h : K * h + K]
            us[2 * m + h, :, 128:256] = low[K * h : K * h + K]
        return carry

    def row_side(b, carry):
        off = pl.multiple_of(b * K, K)
        high, low = split(turned[pl.ds(off, K), :])
        weights = jnp.concatenate([high, low, high, jnp.zeros_like(high)], axis=0)
        first = lax.rem(rows[b], nodes)
        second = lax.rem(rows[b + 128], nodes)
        both = dot16(jnp.concatenate([us[first], us[second]], axis=0), weights)
        turned[pl.ds(off, K), :] = jnp.where(left, both[:K], both[K:])
        return carry

    def expand_cols(q, carry):
        s = q // half
        m = q % half
        pair = win[s, m]
        rolled = pltpu.roll(pair, K, 1)
        for h, (a, b) in enumerate(((pair, rolled), (rolled, pair))):
            for ref, value in ((lw, jnp.where(left, a, 0.0)), (rw, jnp.where(left, 0.0, b))):
                high, low = split(value)
                ref[2 * q + h, :, 0:128] = high
                ref[2 * q + h, :, 128:256] = low
        return carry

    def col_side(b, carry):
        off = pl.multiple_of(b * K, K)
        high, low = split(turned[pl.ds(off, K), :])
        first = jnp.clip(cols[b] - (leaf - REACH) * nodes, 0, last)
        second = jnp.clip(cols[b + 128] - (leaf - REACH) * nodes, 0, last)
        weights = jnp.concatenate([lw[first], rw[second]], axis=0)
        both = dot16(jnp.concatenate([high, low], axis=0), weights)
        turned[pl.ds(off, K), :] = both[:K, :128] + both[K:, :128] + both[:K, 128:]
        return carry

    def run(body, first, past, unroll):
        lax.fori_loop(first, past, body, 0, unroll=unroll)

    pairs = (2 * REACH + 1) * half
    window = []

    def send_window(slot, s, first, count):
        part = pl.ds(first, count)
        copy = send(win.at[REACH, part], win.at[REACH - s, part], ws.at[slot], wr.at[slot], (near(s), dom))
        window.append((copy, REACH - s, first, count))

    sends = [
        [(2, 0, half), (-2, 0, half)],
        [(1, 0, half), (-1, 0, half), (3, 0, half // 2), (-3, 0, half // 2)],
        [(3, half // 2, half // 2), (-3, half // 2, half // 2)],
    ]

    def send_windows(step):
        for what in sends[step]:
            send_window(len(window), *what)

    def prepare():
        for load in index_loads:
            load.wait()
        for arrival in gather:
            arrival.wait_recv()
        send_windows(0)
        run(expand_rows, 0, half, 2)

    def widen(first, past):
        for copy, _, _, _ in window[first:past]:
            copy.wait_recv()
        for _, s, begin, count in window[first:past]:
            run(expand_cols, s * half + begin, s * half + begin + count, 4)

    queues = {"turn": iter(range(K)), "row": iter(range(128)), "col": iter(range(128))}
    bodies = {"turn": turn, "row": row_side, "col": col_side}

    def hook(kind, total):
        def emit(point):
            points = K // 2
            for _ in range(total * (point + 1) // points - total * point // points):
                n = next(queues[kind], None)
                if n is not None:
                    bodies[kind](n, 0)
        return emit if total else None

    def chunk(kind, count, unroll):
        taken = list(itertools.islice(queues[kind], count))
        run(bodies[kind], taken[0], taken[-1] + 1, unroll)

    def fill(stage):
        if stage == 0:
            chunk("turn", TURN_FILL, 4)
            prepare()
        if stage == stages - 3:
            if stage:
                send_windows(1)
                chunk("row", ROW_FILL, 8)
            run(expand_cols, REACH * half, REACH * half + half, 4)
        elif stage == stages - 2:
            if stages < 4:
                send_windows(1)
            send_windows(2)
            chunk("row", None, 8)
            widen(0, 2)
        elif stage == stages - 1:
            widen(2, len(window))
            chunk("col", COL_FILL, 8)

    hooks = {0: ("row", ROW_HOOK, ROW_HOOK), stages - 3: ("row", ROW_HOOK, ROW_HOOK), stages - 1: ("col", COL_HOOK, 128 - COL_FILL - COL_HOOK)}

    child_copy.wait()
    stacked = [child[n] for n in range(per)]
    current = factor([dot(x, x, NT) for x in stacked])
    for m in range(own):
        tall = jnp.concatenate([current[2 * m][:, :K], current[2 * m + 1][:, :K]], axis=0)
        win[REACH, own * dom + m] = tall.T
    pl.semaphore_wait(barrier, len(greeted))
    mine = win.at[REACH, pl.ds(own * dom, own)]
    gather = spread(mine, gs, gr)

    for load in loads:
        load.wait()
    for n in range(3 * stages + 3):
        pair = par[n]
        par[n] = jnp.concatenate([pair[:, :K], pltpu.roll(pair, K, 1)[:, :K]], axis=0).T

    def product(packed, n):
        wide = jnp.concatenate([jnp.where(left, packed, 0.0), jnp.where(left, 0.0, packed)], axis=0)
        return dot(par[n], wide, NT)

    xa = [product(jnp.where(left, current[2 * s], pltpu.roll(current[2 * s + 1], K, 1)), s) for s in range(own)]
    below = current
    coup_copy.wait()
    current = factor([dot(x, x, NT) for x in xa], hook("turn", (K - TURN_FILL) // 2))
    x = product(jnp.where(left, current[0], pltpu.roll(current[1], K, 1)), own)
    for n in range(per):
        bottom_out[n] = dot(inverse(below[n]), stacked[n], NN)
    stores = [pltpu.make_async_copy(bottom_out, bottom_hbm, out_sem.at[0])]
    stores[0].start()
    for s in range(own):
        local_out[own * dom + s] = dot(inverse(current[s]), xa[s], NN)
    arrivals = spread(local_out.at[pl.ds(own * dom, own)], bs, br)
    (factored,) = factor([dot(x, x, NT)], hook("turn", (K - TURN_FILL) // 2))

    top_out[0] = jnp.zeros((K, 128), F32)

    def keep_bases(stage, lowers, xs, top, x):
        if stage == 0:
            for r, (lower, value) in enumerate(zip(lowers + [top], xs + [x])):
                local_out[half + doms + r] = dot(inverse(lower), value, NN)
            return
        first, second, middle = bases[stage - 1]
        at_first, at_middle = first == leaf, middle == leaf
        lower = jnp.where(at_middle, top, jnp.where(at_first, lowers[0], lowers[1]))
        value = jnp.where(at_middle, x, jnp.where(at_first, xs[0], xs[1]))
        found = at_first | at_middle | (second == leaf)
        top_out[0] = jnp.where(found, dot(inverse(lower), value, NN), top_out[0])

    pending = None
    for stage in range(stages):
        spot, others = groups[stage]
        xr[stage, spot] = jnp.where(lax.rem(spot, 2) == 0, factored, pltpu.roll(factored, K, 1))
        view = xr.at[stage, spot]
        copies = [send(view, view, es.at[stage, k], er.at[stage, k], others[k]) for k in range(3)]
        if stage == 0:
            local_out[half + dom] = dot(inverse(factored), x, NN)
            arrivals += spread(local_out.at[pl.ds(half + dom, 1)], cs, cr)
        else:
            keep_bases(*pending)
        fill(stage)
        for copy in copies:
            copy.wait_recv()
        kind, low, high = hooks.get(stage, ("row", 0, 0))
        xs = [product(jnp.where(left, xr[stage, 2 * s], xr[stage, 2 * s + 1]), 3 * stage + 3 + s) for s in range(2)]
        lowers = factor([dot(v, v, NT) for v in xs], hook(kind, low))
        if stage == stages - 1:
            ready = pl.ds(0, (COL_FILL + COL_HOOK) * K)
            stores.append(pltpu.make_async_copy(turned.at[ready], turned_hbm.at[ready], out_sem.at[1]))
            stores[-1].start()
            for copy in arrivals:
                copy.wait_recv()
            stores.append(pltpu.make_async_copy(local_out, local_hbm, out_sem.at[2]))
            stores[-1].start()
        x = product(jnp.where(left, lowers[0], pltpu.roll(lowers[1], K, 1)), 3 * stage + 5)
        (factored,) = factor([dot(x, x, NT)], hook(kind, high))
        pending = (stage, lowers, xs, factored, x)
    if COL_FILL + COL_HOOK < 128:
        ready = pl.ds((COL_FILL + COL_HOOK) * K, (128 - COL_FILL - COL_HOOK) * K)
        stores.append(pltpu.make_async_copy(turned.at[ready], turned_hbm.at[ready], out_sem.at[5]))
        stores[-1].start()
    root_out[...] = factored[:, :K]
    stores.append(pltpu.make_async_copy(root_out, root_hbm, out_sem.at[3]))
    stores[-1].start()
    keep_bases(*pending)
    stores.append(pltpu.make_async_copy(top_out, top_hbm, out_sem.at[4]))
    stores[-1].start()

    for copy in started:
        copy.wait_send()
    for copy in stores:
        copy.wait()


def finish(bottom, local, top, root, turned, bottom_out, local_out, top_out, root_out, proj_out,
           bottom_in, local_in, top_in, root_in, parts_in, ct, load_sem, part_sem, store_sem, out_sem):
    parts, _, deep, _ = parts_in.shape
    part_loads = []
    for part in range(parts):
        copy = pltpu.make_async_copy(turned.at[:, pl.ds(deep * part, deep)], parts_in.at[part], part_sem.at[part])
        copy.start()
        part_loads.append(copy)
    small = ((bottom, bottom_in, bottom_out), (local, local_in, local_out), (top, top_in, top_out), (root, root_in, root_out))
    loads = [pltpu.make_async_copy(src, mid, load_sem.at[n]) for n, (src, mid, _) in enumerate(small)]
    stores = [pltpu.make_async_copy(mid, dst, store_sem.at[n]) for n, (_, mid, dst) in enumerate(small)]
    for load in loads:
        load.start()
    for part in range(parts):
        part_loads[part].wait()
        for r in range(deep):
            slab = parts_in[part, :, r, :].T
            ct[deep * part + r, :, 0:128] = slab[:K]
            ct[deep * part + r, :, 128:256] = slab[K:]
        span = pl.ds(deep * part, deep)
        copy = pltpu.make_async_copy(ct.at[span], proj_out.at[span], out_sem.at[part])
        copy.start()
        stores.append(copy)
        if part == 0:
            for load, store in zip(loads, stores):
                load.wait()
                store.start()
    for copy in stores:
        copy.wait()


def on_device(doms, leaves, child_terms, transfer, top_transfer, coupling, block_row, block_col):
    per = child_terms.shape[0]
    nodes = per * doms
    top_levels = leaves.bit_length() - 1
    stages = (top_levels + doms.bit_length() - 1) // 2
    hbm = pl.BlockSpec(memory_space=pltpu.HBM)
    dma = pltpu.SemaphoreType.DMA
    sides = 2 * REACH
    small_shapes = ((per, K, 2 * K), (nodes - 1, K, 2 * K), (1, K, 2 * K), (K, K))
    small = tuple(jax.ShapeDtypeStruct(shape, F32) for shape in small_shapes)
    small_scratch = [pltpu.VMEM(shape, F32) for shape in small_shapes]
    *ready, turned = pl.pallas_call(
        functools.partial(kernel, doms, leaves),
        out_shape=small + (jax.ShapeDtypeStruct((128 * K, 128), F32),),
        in_specs=[hbm] * 6,
        out_specs=(hbm,) * 5,
        scratch_shapes=small_scratch + [
            pltpu.VMEM((128 * K, 128), F32),
            pltpu.VMEM((per, K, 128), F32),
            pltpu.SMEM((256,), jnp.int32),
            pltpu.SMEM((256,), jnp.int32),
            pltpu.VMEM((sides + 1, nodes // 2, K, 128), F32),
            pltpu.VMEM((K, K, 256), F32),
            pltpu.VMEM((3 * stages + 3, K, 128), F32),
            pltpu.VMEM((nodes, K, 256), BF),
            pltpu.VMEM(((sides + 1) * nodes, K, 256), BF),
            pltpu.VMEM(((sides + 1) * nodes, K, 256), BF),
            pltpu.VMEM((stages, 4, K, 128), F32),
            dma((3 * stages + 4,)),
            dma((6,)),
            dma((doms - 1,)), dma((doms - 1,)),
            dma((8,)), dma((8,)),
            dma((doms - 1,)), dma((doms - 1,)),
            dma((doms - 1,)), dma((doms - 1,)),
            dma((stages, 3)), dma((stages, 3)),
        ],
        compiler_params=pltpu.CompilerParams(
            collective_id=0, has_side_effects=True, vmem_limit_bytes=60 * 2**20),
    )(child_terms, transfer, top_transfer, jnp.transpose(coupling, (1, 2, 0)), block_row, block_col)
    bottom, local, top, root, projected = pl.pallas_call(
        finish,
        out_shape=small + (jax.ShapeDtypeStruct((K, K, 256), F32),),
        in_specs=[hbm] * 5,
        out_specs=(hbm,) * 5,
        scratch_shapes=small_scratch + [
            pltpu.VMEM((4, 128, K // 4, 128), F32), pltpu.VMEM((K, K, 256), F32),
            dma((4,)), dma((4,)), dma((4,)), dma((4,)),
        ],
        compiler_params=pltpu.CompilerParams(vmem_limit_bytes=60 * 2**20),
    )(*ready, turned.reshape(128, K, 128))
    return bottom, local, top, root, jnp.transpose(projected, (2, 0, 1))


def solution(mesh):
    split_all = P(("leaf", "dom"), None, None)
    placed = (split_all, P("leaf", None, None), P(), split_all, P(("leaf", "dom")), P(("leaf", "dom")))
    return jax.shard_map(
        functools.partial(on_device, mesh.shape["dom"], mesh.shape["leaf"]),
        mesh=mesh,
        in_specs=placed,
        out_specs=(split_all, P("leaf", None, None), P("leaf", None, None), P(), split_all),
        check_vma=False,
    )
```

```python
import functools
import itertools

import jax
import jax.numpy as jnp
from jax import lax
from jax.experimental import pallas as pl
from jax.experimental.pallas import tpu as pltpu
from jax.sharding import PartitionSpec as P

REACH = 3
K = 64
F32 = jnp.float32
BF = jnp.bfloat16
HIGH = lax.Precision.HIGHEST
MESH = pl.DeviceIdType.MESH
NN = ((1,), (0,))
NT = ((1,), (1,))


def dot(a, b, dims):
    return lax.dot_general(a, b, (dims, ((), ())), precision=HIGH, preferred_element_type=F32)


def dot16(a, b):
    return lax.dot_general(a, b, (NN, ((), ())), preferred_element_type=F32)


def split(x):
    high = x.astype(BF)
    return high, (x - high.astype(F32)).astype(BF)


TURN_FILL = 32
ROW_FILL = 48
ROW_HOOK = 16
COL_FILL = 48
COL_HOOK = 48


def factor(grams, hook=None):
    double = len(grams) == 1
    WIDE = 16 if len(grams) < 4 else 8
    full = (WIDE, 128)
    sub = lax.broadcasted_iota(jnp.int32, full, 0)
    row = lax.broadcasted_iota(jnp.int32, (K, K), 0)
    col = lax.broadcasted_iota(jnp.int32, (K, K), 1)
    eye = jnp.where(row == col, 1.0, 0.0).astype(F32)
    rests = [jnp.concatenate([g, eye], axis=1) for g in grams]
    dones = [[] for _ in grams]

    def spread_row(value, k):
        return jnp.broadcast_to(value[k : k + 1, :], full)

    for p in range(K // WIDE):
        states = []
        for rest in rests:
            panel = rest[:WIDE]
            cols = [jnp.broadcast_to(panel[:, c : c + 1], full) for c in range(WIDE * p, WIDE * p + WIDE)]
            states.append([panel, cols, jnp.zeros(full, F32)])
        for k in range(0, WIDE, 2 if double else 1):
            here, below = sub == k, sub == k + 1
            both = here | below
            for state in states:
                panel, cols, out = state
                if not double:
                    pivot_row = spread_row(panel, k)
                    heads = [spread_row(c, k) for c in cols[k:]]
                    state[2] = jnp.where(here, pivot_row * lax.rsqrt(heads[0]), out)
                    scale = jnp.where(here, -1.0, cols[k]) * (1.0 / heads[0])
                    state[0] = jnp.where(here, 0.0, panel) - scale * pivot_row
                    for c in range(k + 1, WIDE):
                        cols[c] = jnp.where(here, 0.0, cols[c]) - scale * heads[c - k]
                    continue
                row0, row1 = spread_row(panel, k), spread_row(panel, k + 1)
                tops = [spread_row(c, k) for c in cols[k:]]
                nexts = [spread_row(c, k + 1) for c in cols[k:]]
                inv0 = 1.0 / tops[0]
                down, right = nexts[0] * inv0, tops[1] * inv0
                pivot1 = nexts[1] - down * tops[1]
                inv1 = 1.0 / pivot1
                first = jnp.where(here, -1.0, jnp.where(below, 0.0, cols[k]))
                second = jnp.where(below, -1.0, jnp.where(here, 0.0, cols[k + 1]))
                scale0 = first * inv0
                scale1 = (second - right * first) * inv1
                reduced = row1 - down * row0
                state[2] = jnp.where(here, row0 * lax.rsqrt(tops[0]), jnp.where(below, reduced * lax.rsqrt(pivot1), out))
                state[0] = (jnp.where(both, 0.0, panel) - scale0 * row0) - scale1 * reduced
                for c in range(k + 2, WIDE):
                    rest_col = nexts[c - k] - down * tops[c - k]
                    cols[c] = (jnp.where(both, 0.0, cols[c]) - scale0 * tops[c - k]) - scale1 * rest_col
            if hook is not None and (double or k % 2):
                hook((p * WIDE + k) // 2)
        for n, (panel, _, out) in enumerate(states):
            dones[n].append(out)
            tail = rests[n][WIDE:]
            height = tail.shape[0]
            if height:
                terms = [
                    jnp.broadcast_to(tail[:, c : c + 1], (height, 128)) * jnp.broadcast_to(panel[k : k + 1, :], (height, 128))
                    for k, c in enumerate(range(WIDE * p, WIDE * p + WIDE))
                ]
                while len(terms) > 1:
                    terms = [x + y for x, y in zip(terms[0::2], terms[1::2])]
                rests[n] = tail - terms[0]
    keep = lax.broadcasted_iota(jnp.int32, (K, 128), 1) >= lax.broadcasted_iota(jnp.int32, (K, 128), 0)
    return [jnp.where(keep, jnp.concatenate(done, axis=0), 0.0) for done in dones]


def kernel(doms, leaves, child_hbm, transfer, toptr, coup, rows_hbm, cols_hbm,
           bottom_hbm, local_hbm, top_hbm, root_hbm, turned_hbm,
           bottom_out, local_out, top_out, root_out, turned,
           child, rows, cols, win, ct, par, us, lw, rw, xr,
           in_sem, out_sem, gs, gr, ws, wr, bs, br, cs, cr, es, er):
    leaf = lax.axis_index("leaf")
    dom = lax.axis_index("dom")
    top_levels = leaves.bit_length() - 1
    dom_levels = doms.bit_length() - 1
    stages = (top_levels + dom_levels) // 2
    per = child.shape[0]
    nodes = per * doms
    half = nodes // 2
    own = per // 2
    last = (2 * REACH + 1) * nodes - 1

    child_copy = pltpu.make_async_copy(child_hbm, child, in_sem.at[0])
    child_copy.start()
    loads = [
        pltpu.make_async_copy(transfer.at[pl.ds(own * dom, own)], par.at[pl.ds(0, own)], in_sem.at[1]),
        pltpu.make_async_copy(transfer.at[pl.ds(half + dom, 1)], par.at[pl.ds(2, 1)], in_sem.at[2]),
        pltpu.make_async_copy(transfer.at[pl.ds(half + doms, 3)], par.at[pl.ds(3, 3)], in_sem.at[3]),
    ]
    bases = []
    for t in range(stages - 1):
        step = 4**t
        base = leaf // (4 * step) * (4 * step)
        bases.append([base + step * r for r in (1, 3, 2)])
        for r in range(3):
            n = 3 * (t + 2) + r
            loads.append(pltpu.make_async_copy(toptr.at[pl.ds(bases[t][r], 1)], par.at[pl.ds(n, 1)], in_sem.at[n - 2]))
    for load in loads:
        load.start()
    index_loads = [
        pltpu.make_async_copy(rows_hbm, rows, in_sem.at[3 * stages + 1]),
        pltpu.make_async_copy(cols_hbm, cols, in_sem.at[3 * stages + 2]),
    ]
    for load in index_loads:
        load.start()
    coup_copy = pltpu.make_async_copy(coup, ct, in_sem.at[3 * stages + 3])
    coup_copy.start()

    def near(step):
        return lax.rem(leaf + step + leaves, leaves)

    def dom_peer(step):
        return (leaf, lax.rem(dom + step, doms))

    steps = [s for s in range(-REACH, REACH + 1) if s]
    groups = [(dom, [dom_peer(k) for k in range(1, 4)])]
    for t in range(stages - 1):
        step = 4**t
        spot = lax.rem(leaf // step, 4)
        groups.append((spot, [(leaf + (lax.rem(spot + k, 4) - spot) * step, dom) for k in range(1, 4)]))
    greeted = [(near(s), dom) for s in steps]
    for _, others in groups:
        greeted += others
    barrier = pltpu.get_barrier_semaphore()
    for other in greeted:
        pl.semaphore_signal(barrier, inc=1, device_id=other, device_id_type=MESH)

    lane = lax.broadcasted_iota(jnp.int32, (K, 128), 1)
    left = lane < K
    started = []

    def send(src, dst, send_sem, recv_sem, other):
        copy = pltpu.make_async_remote_copy(
            src_ref=src, dst_ref=dst, send_sem=send_sem, recv_sem=recv_sem,
            device_id=other, device_id_type=MESH)
        copy.start()
        started.append(copy)
        return copy

    def spread(view, send_sems, recv_sems):
        return [send(view, view, send_sems.at[k - 1], recv_sems.at[k - 1], dom_peer(k)) for k in range(1, doms)]

    def inverse(factored):
        return pltpu.roll(factored, K, 1)[:, :K]

    def turn(i, carry):
        slab = jnp.concatenate([ct[i, :, 0:128], ct[i, :, 128:256]], axis=0)
        turned[pl.ds(i, 128, K), :] = slab.T
        return carry

    def expand_rows(m, carry):
        pair = win[REACH, m]
        both = jnp.concatenate([pair, pair], axis=0).T
        high = both.astype(BF)
        low = jnp.where(lax.broadcasted_iota(jnp.int32, (128, 128), 1) < K, both - high.astype(F32), 0.0).astype(BF)
        for h in range(2):
            us[2 * m + h, :, 0:128] = high[K * h : K * h + K]
            us[2 * m + h, :, 128:256] = low[K * h : K * h + K]
        return carry

    def row_side(b, carry):
        off = pl.multiple_of(b * K, K)
        high, low = split(turned[pl.ds(off, K), :])
        weights = jnp.concatenate([high, low, high, jnp.zeros_like(high)], axis=0)
        first = lax.rem(rows[b], nodes)
        second = lax.rem(rows[b + 128], nodes)
        both = dot16(jnp.concatenate([us[first], us[second]], axis=0), weights)
        turned[pl.ds(off, K), :] = jnp.where(left, both[:K], both[K:])
        return carry

    def expand_cols(q, carry):
        s = q // half
        m = q % half
        pair = win[s, m]
        rolled = pltpu.roll(pair, K, 1)
        for h, (a, b) in enumerate(((pair, rolled), (rolled, pair))):
            for ref, value in ((lw, jnp.where(left, a, 0.0)), (rw, jnp.where(left, 0.0, b))):
                high, low = split(value)
                ref[2 * q + h, :, 0:128] = high
                ref[2 * q + h, :, 128:256] = low
        return carry

    def col_side(b, carry):
        off = pl.multiple_of(b * K, K)
        high, low = split(turned[pl.ds(off, K), :])
        first = jnp.clip(cols[b] - (leaf - REACH) * nodes, 0, last)
        second = jnp.clip(cols[b + 128] - (leaf - REACH) * nodes, 0, last)
        weights = jnp.concatenate([lw[first], rw[second]], axis=0)
        both = dot16(jnp.concatenate([high, low], axis=0), weights)
        turned[pl.ds(off, K), :] = both[:K, :128] + both[K:, :128] + both[:K, 128:]
        return carry

    def run(body, first, past, unroll):
        lax.fori_loop(first, past, body, 0, unroll=unroll)

    pairs = (2 * REACH + 1) * half
    window = []

    def send_window(slot, s, first, count):
        part = pl.ds(first, count)
        copy = send(win.at[REACH, part], win.at[REACH - s, part], ws.at[slot], wr.at[slot], (near(s), dom))
        window.append((copy, REACH - s, first, count))

    sends = [
        [(2, 0, half), (-2, 0, half)],
        [(1, 0, half), (-1, 0, half), (3, 0, half // 2), (-3, 0, half // 2)],
        [(3, half // 2, half // 2), (-3, half // 2, half // 2)],
    ]

    def send_windows(step):
        for what in sends[step]:
            send_window(len(window), *what)

    def prepare():
        for load in index_loads:
            load.wait()
        for arrival in gather:
            arrival.wait_recv()
        send_windows(0)
        run(expand_rows, 0, half, 2)

    def widen(first, past):
        for copy, _, _, _ in window[first:past]:
            copy.wait_recv()
        for _, s, begin, count in window[first:past]:
            run(expand_cols, s * half + begin, s * half + begin + count, 4)

    queues = {"turn": iter(range(K)), "row": iter(range(128)), "col": iter(range(128))}
    bodies = {"turn": turn, "row": row_side, "col": col_side}

    def hook(kind, total):
        def emit(point):
            points = K // 2
            for _ in range(total * (point + 1) // points - total * point // points):
                n = next(queues[kind], None)
                if n is not None:
                    bodies[kind](n, 0)
        return emit if total else None

    def chunk(kind, count, unroll):
        taken = list(itertools.islice(queues[kind], count))
        run(bodies[kind], taken[0], taken[-1] + 1, unroll)

    def fill(stage):
        if stage == 0:
            chunk("turn", TURN_FILL, 4)
            prepare()
        if stage == stages - 3:
            if stage:
                send_windows(1)
                chunk("row", ROW_FILL, 8)
            run(expand_cols, REACH * half, REACH * half + half, 4)
        elif stage == stages - 2:
            if stages < 4:
                send_windows(1)
            send_windows(2)
            chunk("row", None, 8)
            widen(0, 2)
        elif stage == stages - 1:
            widen(2, len(window))
            chunk("col", COL_FILL, 8)

    hooks = {0: ("row", ROW_HOOK, ROW_HOOK), stages - 3: ("row", ROW_HOOK, ROW_HOOK), stages - 1: ("col", COL_HOOK, 128 - COL_FILL - COL_HOOK)}

    child_copy.wait()
    stacked = [child[n] for n in range(per)]
    current = factor([dot(x, x, NT) for x in stacked])
    for m in range(own):
        tall = jnp.concatenate([current[2 * m][:, :K], current[2 * m + 1][:, :K]], axis=0)
        win[REACH, own * dom + m] = tall.T
    pl.semaphore_wait(barrier, len(greeted))
    mine = win.at[REACH, pl.ds(own * dom, own)]
    gather = spread(mine, gs, gr)

    for load in loads:
        load.wait()
    for n in range(3 * stages + 3):
        pair = par[n]
        par[n] = jnp.concatenate([pair[:, :K], pltpu.roll(pair, K, 1)[:, :K]], axis=0).T

    def product(packed, n):
        wide = jnp.concatenate([jnp.where(left, packed, 0.0), jnp.where(left, 0.0, packed)], axis=0)
        return dot(par[n], wide, NT)

    xa = [product(jnp.where(left, current[2 * s], pltpu.roll(current[2 * s + 1], K, 1)), s) for s in range(own)]
    below = current
    coup_copy.wait()
    current = factor([dot(x, x, NT) for x in xa], hook("turn", (K - TURN_FILL) // 2))
    x = product(jnp.where(left, current[0], pltpu.roll(current[1], K, 1)), own)
    for n in range(per):
        bottom_out[n] = dot(inverse(below[n]), stacked[n], NN)
    stores = [pltpu.make_async_copy(bottom_out, bottom_hbm, out_sem.at[0])]
    stores[0].start()
    for s in range(own):
        local_out[own * dom + s] = dot(inverse(current[s]), xa[s], NN)
    arrivals = spread(local_out.at[pl.ds(own * dom, own)], bs, br)
    (factored,) = factor([dot(x, x, NT)], hook("turn", (K - TURN_FILL) // 2))

    top_out[0] = jnp.zeros((K, 128), F32)

    def keep_bases(stage, lowers, xs, top, x):
        if stage == 0:
            for r, (lower, value) in enumerate(zip(lowers + [top], xs + [x])):
                local_out[half + doms + r] = dot(inverse(lower), value, NN)
            return
        first, second, middle = bases[stage - 1]
        at_first, at_middle = first == leaf, middle == leaf
        lower = jnp.where(at_middle, top, jnp.where(at_first, lowers[0], lowers[1]))
        value = jnp.where(at_middle, x, jnp.where(at_first, xs[0], xs[1]))
        found = at_first | at_middle | (second == leaf)
        top_out[0] = jnp.where(found, dot(inverse(lower), value, NN), top_out[0])

    pending = None
    for stage in range(stages):
        spot, others = groups[stage]
        xr[stage, spot] = jnp.where(lax.rem(spot, 2) == 0, factored, pltpu.roll(factored, K, 1))
        view = xr.at[stage, spot]
        copies = [send(view, view, es.at[stage, k], er.at[stage, k], others[k]) for k in range(3)]
        if stage == 0:
            local_out[half + dom] = dot(inverse(factored), x, NN)
            arrivals += spread(local_out.at[pl.ds(half + dom, 1)], cs, cr)
        else:
            keep_bases(*pending)
        fill(stage)
        for copy in copies:
            copy.wait_recv()
        kind, low, high = hooks.get(stage, ("row", 0, 0))
        xs = [product(jnp.where(left, xr[stage, 2 * s], xr[stage, 2 * s + 1]), 3 * stage + 3 + s) for s in range(2)]
        lowers = factor([dot(v, v, NT) for v in xs], hook(kind, low))
        if stage == stages - 1:
            ready = pl.ds(0, (COL_FILL + COL_HOOK) * K)
            stores.append(pltpu.make_async_copy(turned.at[ready], turned_hbm.at[ready], out_sem.at[1]))
            stores[-1].start()
            for copy in arrivals:
                copy.wait_recv()
            stores.append(pltpu.make_async_copy(local_out, local_hbm, out_sem.at[2]))
            stores[-1].start()
        x = product(jnp.where(left, lowers[0], pltpu.roll(lowers[1], K, 1)), 3 * stage + 5)
        (factored,) = factor([dot(x, x, NT)], hook(kind, high))
        pending = (stage, lowers, xs, factored, x)
    if COL_FILL + COL_HOOK < 128:
        ready = pl.ds((COL_FILL + COL_HOOK) * K, (128 - COL_FILL - COL_HOOK) * K)
        stores.append(pltpu.make_async_copy(turned.at[ready], turned_hbm.at[ready], out_sem.at[5]))
        stores[-1].start()
    root_out[...] = factored[:, :K]
    stores.append(pltpu.make_async_copy(root_out, root_hbm, out_sem.at[3]))
    stores[-1].start()
    keep_bases(*pending)
    stores.append(pltpu.make_async_copy(top_out, top_hbm, out_sem.at[4]))
    stores[-1].start()

    for copy in started:
        copy.wait_send()
    for copy in stores:
        copy.wait()


def finish(bottom, local, top, root, turned, bottom_out, local_out, top_out, root_out, proj_out,
           bottom_in, local_in, top_in, root_in, parts_in, ct, load_sem, part_sem, store_sem, out_sem):
    parts, _, deep, _ = parts_in.shape
    part_loads = []
    for part in range(parts):
        copy = pltpu.make_async_copy(turned.at[:, pl.ds(deep * part, deep)], parts_in.at[part], part_sem.at[part])
        copy.start()
        part_loads.append(copy)
    small = ((bottom, bottom_in, bottom_out), (local, local_in, local_out), (top, top_in, top_out), (root, root_in, root_out))
    loads = [pltpu.make_async_copy(src, mid, load_sem.at[n]) for n, (src, mid, _) in enumerate(small)]
    stores = [pltpu.make_async_copy(mid, dst, store_sem.at[n]) for n, (_, mid, dst) in enumerate(small)]
    for load in loads:
        load.start()
    for part in range(parts):
        part_loads[part].wait()
        for r in range(deep):
            slab = parts_in[part, :, r, :].T
            ct[deep * part + r, :, 0:128] = slab[:K]
            ct[deep * part + r, :, 128:256] = slab[K:]
        span = pl.ds(deep * part, deep)
        copy = pltpu.make_async_copy(ct.at[span], proj_out.at[span], out_sem.at[part])
        copy.start()
        stores.append(copy)
        if part == 0:
            for load, store in zip(loads, stores):
                load.wait()
                store.start()
    for copy in stores:
        copy.wait()


def on_device(doms, leaves, child_terms, transfer, top_transfer, coupling, block_row, block_col):
    per = child_terms.shape[0]
    nodes = per * doms
    top_levels = leaves.bit_length() - 1
    stages = (top_levels + doms.bit_length() - 1) // 2
    hbm = pl.BlockSpec(memory_space=pltpu.HBM)
    dma = pltpu.SemaphoreType.DMA
    sides = 2 * REACH
    small_shapes = ((per, K, 2 * K), (nodes - 1, K, 2 * K), (1, K, 2 * K), (K, K))
    small = tuple(jax.ShapeDtypeStruct(shape, F32) for shape in small_shapes)
    small_scratch = [pltpu.VMEM(shape, F32) for shape in small_shapes]
    *ready, turned = pl.pallas_call(
        functools.partial(kernel, doms, leaves),
        out_shape=small + (jax.ShapeDtypeStruct((128 * K, 128), F32),),
        in_specs=[hbm] * 6,
        out_specs=(hbm,) * 5,
        scratch_shapes=small_scratch + [
            pltpu.VMEM((128 * K, 128), F32),
            pltpu.VMEM((per, K, 128), F32),
            pltpu.SMEM((256,), jnp.int32),
            pltpu.SMEM((256,), jnp.int32),
            pltpu.VMEM((sides + 1, nodes // 2, K, 128), F32),
            pltpu.VMEM((K, K, 256), F32),
            pltpu.VMEM((3 * stages + 3, K, 128), F32),
            pltpu.VMEM((nodes, K, 256), BF),
            pltpu.VMEM(((sides + 1) * nodes, K, 256), BF),
            pltpu.VMEM(((sides + 1) * nodes, K, 256), BF),
            pltpu.VMEM((stages, 4, K, 128), F32),
            dma((3 * stages + 4,)),
            dma((6,)),
            dma((doms - 1,)), dma((doms - 1,)),
            dma((8,)), dma((8,)),
            dma((doms - 1,)), dma((doms - 1,)),
            dma((doms - 1,)), dma((doms - 1,)),
            dma((stages, 3)), dma((stages, 3)),
        ],
        compiler_params=pltpu.CompilerParams(
            collective_id=0, has_side_effects=True, vmem_limit_bytes=60 * 2**20),
    )(child_terms, transfer, top_transfer, jnp.transpose(coupling, (1, 2, 0)), block_row, block_col)
    bottom, local, top, root, projected = pl.pallas_call(
        finish,
        out_shape=small + (jax.ShapeDtypeStruct((K, K, 256), F32),),
        in_specs=[hbm] * 5,
        out_specs=(hbm,) * 5,
        scratch_shapes=small_scratch + [
            pltpu.VMEM((4, 128, K // 4, 128), F32), pltpu.VMEM((K, K, 256), F32),
            dma((4,)), dma((4,)), dma((4,)), dma((4,)),
        ],
        compiler_params=pltpu.CompilerParams(vmem_limit_bytes=60 * 2**20),
    )(*ready, turned.reshape(128, K, 128))
    return bottom, local, top, root, jnp.transpose(projected, (2, 0, 1))


def solution(mesh):
    split_all = P(("leaf", "dom"), None, None)
    placed = (split_all, P("leaf", None, None), P(), split_all, P(("leaf", "dom")), P(("leaf", "dom")))
    return jax.shard_map(
        functools.partial(on_device, mesh.shape["dom"], mesh.shape["leaf"]),
        mesh=mesh,
        in_specs=placed,
        out_specs=(split_all, P("leaf", None, None), P("leaf", None, None), P(), split_all),
        check_vma=False,
    )
```

```python
import functools
import itertools

import jax
import jax.numpy as jnp
from jax import lax
from jax.experimental import pallas as pl
from jax.experimental.pallas import tpu as pltpu
from jax.sharding import PartitionSpec as P

REACH = 3
K = 64
F32 = jnp.float32
BF = jnp.bfloat16
HIGH = lax.Precision.HIGHEST
MESH = pl.DeviceIdType.MESH
NN = ((1,), (0,))
NT = ((1,), (1,))


def dot(a, b, dims):
    return lax.dot_general(a, b, (dims, ((), ())), precision=HIGH, preferred_element_type=F32)


def dot16(a, b):
    return lax.dot_general(a, b, (NN, ((), ())), preferred_element_type=F32)


def split(x):
    high = x.astype(BF)
    return high, (x - high.astype(F32)).astype(BF)


TURN_FILL = 32
ROW_FILL = 48
ROW_HOOK = 16
COL_FILL = 48
COL_HOOK = 48


def factor(grams, hook=None):
    double = len(grams) == 1
    WIDE = 16 if len(grams) < 4 else 8
    full = (WIDE, 128)
    sub = lax.broadcasted_iota(jnp.int32, full, 0)
    row = lax.broadcasted_iota(jnp.int32, (K, K), 0)
    col = lax.broadcasted_iota(jnp.int32, (K, K), 1)
    eye = jnp.where(row == col, 1.0, 0.0).astype(F32)
    rests = [jnp.concatenate([g, eye], axis=1) for g in grams]
    dones = [[] for _ in grams]

    def spread_row(value, k):
        return jnp.broadcast_to(value[k : k + 1, :], full)

    for p in range(K // WIDE):
        states = []
        for rest in rests:
            panel = rest[:WIDE]
            cols = [jnp.broadcast_to(panel[:, c : c + 1], full) for c in range(WIDE * p, WIDE * p + WIDE)]
            states.append([panel, cols, jnp.zeros(full, F32)])
        for k in range(0, WIDE, 2 if double else 1):
            here, below = sub == k, sub == k + 1
            both = here | below
            for state in states:
                panel, cols, out = state
                if not double:
                    pivot_row = spread_row(panel, k)
                    heads = [spread_row(c, k) for c in cols[k:]]
                    state[2] = jnp.where(here, pivot_row * lax.rsqrt(heads[0]), out)
                    scale = jnp.where(here, -1.0, cols[k]) * (1.0 / heads[0])
                    state[0] = jnp.where(here, 0.0, panel) - scale * pivot_row
                    for c in range(k + 1, WIDE):
                        cols[c] = jnp.where(here, 0.0, cols[c]) - scale * heads[c - k]
                    continue
                row0, row1 = spread_row(panel, k), spread_row(panel, k + 1)
                tops = [spread_row(c, k) for c in cols[k:]]
                nexts = [spread_row(c, k + 1) for c in cols[k:]]
                inv0 = 1.0 / tops[0]
                down, right = nexts[0] * inv0, tops[1] * inv0
                pivot1 = nexts[1] - down * tops[1]
                inv1 = 1.0 / pivot1
                first = jnp.where(here, -1.0, jnp.where(below, 0.0, cols[k]))
                second = jnp.where(below, -1.0, jnp.where(here, 0.0, cols[k + 1]))
                scale0 = first * inv0
                scale1 = (second - right * first) * inv1
                reduced = row1 - down * row0
                state[2] = jnp.where(here, row0 * lax.rsqrt(tops[0]), jnp.where(below, reduced * lax.rsqrt(pivot1), out))
                state[0] = (jnp.where(both, 0.0, panel) - scale0 * row0) - scale1 * reduced
                for c in range(k + 2, WIDE):
                    rest_col = nexts[c - k] - down * tops[c - k]
                    cols[c] = (jnp.where(both, 0.0, cols[c]) - scale0 * tops[c - k]) - scale1 * rest_col
            if hook is not None and (double or k % 2):
                hook((p * WIDE + k) // 2)
        for n, (panel, _, out) in enumerate(states):
            dones[n].append(out)
            tail = rests[n][WIDE:]
            height = tail.shape[0]
            if height:
                terms = [
                    jnp.broadcast_to(tail[:, c : c + 1], (height, 128)) * jnp.broadcast_to(panel[k : k + 1, :], (height, 128))
                    for k, c in enumerate(range(WIDE * p, WIDE * p + WIDE))
                ]
                while len(terms) > 1:
                    terms = [x + y for x, y in zip(terms[0::2], terms[1::2])]
                rests[n] = tail - terms[0]
    keep = lax.broadcasted_iota(jnp.int32, (K, 128), 1) >= lax.broadcasted_iota(jnp.int32, (K, 128), 0)
    return [jnp.where(keep, jnp.concatenate(done, axis=0), 0.0) for done in dones]


def kernel(doms, leaves, child_hbm, transfer, toptr, coup, rows_hbm, cols_hbm,
           bottom_hbm, local_hbm, top_hbm, root_hbm, turned_hbm,
           bottom_out, local_out, top_out, root_out, turned,
           child, rows, cols, win, ct, par, us, lw, rw, xr,
           in_sem, out_sem, gs, gr, ws, wr, bs, br, cs, cr, es, er):
    leaf = lax.axis_index("leaf")
    dom = lax.axis_index("dom")
    top_levels = leaves.bit_length() - 1
    dom_levels = doms.bit_length() - 1
    stages = (top_levels + dom_levels) // 2
    per = child.shape[0]
    nodes = per * doms
    half = nodes // 2
    own = per // 2
    last = (2 * REACH + 1) * nodes - 1

    child_copy = pltpu.make_async_copy(child_hbm, child, in_sem.at[0])
    child_copy.start()
    loads = [
        pltpu.make_async_copy(transfer.at[pl.ds(own * dom, own)], par.at[pl.ds(0, own)], in_sem.at[1]),
        pltpu.make_async_copy(transfer.at[pl.ds(half + dom, 1)], par.at[pl.ds(2, 1)], in_sem.at[2]),
        pltpu.make_async_copy(transfer.at[pl.ds(half + doms, 3)], par.at[pl.ds(3, 3)], in_sem.at[3]),
    ]
    bases = []
    for t in range(stages - 1):
        step = 4**t
        base = leaf // (4 * step) * (4 * step)
        bases.append([base + step * r for r in (1, 3, 2)])
        for r in range(3):
            n = 3 * (t + 2) + r
            loads.append(pltpu.make_async_copy(toptr.at[pl.ds(bases[t][r], 1)], par.at[pl.ds(n, 1)], in_sem.at[n - 2]))
    for load in loads:
        load.start()
    index_loads = [
        pltpu.make_async_copy(rows_hbm, rows, in_sem.at[3 * stages + 1]),
        pltpu.make_async_copy(cols_hbm, cols, in_sem.at[3 * stages + 2]),
    ]
    for load in index_loads:
        load.start()
    coup_copy = pltpu.make_async_copy(coup, ct, in_sem.at[3 * stages + 3])
    coup_copy.start()

    def near(step):
        return lax.rem(leaf + step + leaves, leaves)

    def dom_peer(step):
        return (leaf, lax.rem(dom + step, doms))

    steps = [s for s in range(-REACH, REACH + 1) if s]
    groups = [(dom, [dom_peer(k) for k in range(1, 4)])]
    for t in range(stages - 1):
        step = 4**t
        spot = lax.rem(leaf // step, 4)
        groups.append((spot, [(leaf + (lax.rem(spot + k, 4) - spot) * step, dom) for k in range(1, 4)]))
    greeted = [(near(s), dom) for s in steps]
    for _, others in groups:
        greeted += others
    barrier = pltpu.get_barrier_semaphore()
    for other in greeted:
        pl.semaphore_signal(barrier, inc=1, device_id=other, device_id_type=MESH)

    lane = lax.broadcasted_iota(jnp.int32, (K, 128), 1)
    left = lane < K
    started = []

    def send(src, dst, send_sem, recv_sem, other):
        copy = pltpu.make_async_remote_copy(
            src_ref=src, dst_ref=dst, send_sem=send_sem, recv_sem=recv_sem,
            device_id=other, device_id_type=MESH)
        copy.start()
        started.append(copy)
        return copy

    def spread(view, send_sems, recv_sems):
        return [send(view, view, send_sems.at[k - 1], recv_sems.at[k - 1], dom_peer(k)) for k in range(1, doms)]

    def inverse(factored):
        return pltpu.roll(factored, K, 1)[:, :K]

    def turn(i, carry):
        slab = jnp.concatenate([ct[i, :, 0:128], ct[i, :, 128:256]], axis=0)
        turned[pl.ds(i, 128, K), :] = slab.T
        return carry

    def expand_rows(m, carry):
        pair = win[REACH, m]
        both = jnp.concatenate([pair, pair], axis=0).T
        high = both.astype(BF)
        low = jnp.where(lax.broadcasted_iota(jnp.int32, (128, 128), 1) < K, both - high.astype(F32), 0.0).astype(BF)
        for h in range(2):
            us[2 * m + h, :, 0:128] = high[K * h : K * h + K]
            us[2 * m + h, :, 128:256] = low[K * h : K * h + K]
        return carry

    def row_side(b, carry):
        off = pl.multiple_of(b * K, K)
        high, low = split(turned[pl.ds(off, K), :])
        weights = jnp.concatenate([high, low, high, jnp.zeros_like(high)], axis=0)
        first = lax.rem(rows[b], nodes)
        second = lax.rem(rows[b + 128], nodes)
        both = dot16(jnp.concatenate([us[first], us[second]], axis=0), weights)
        turned[pl.ds(off, K), :] = jnp.where(left, both[:K], both[K:])
        return carry

    def expand_cols(q, carry):
        s = q // half
        m = q % half
        pair = win[s, m]
        rolled = pltpu.roll(pair, K, 1)
        for h, (a, b) in enumerate(((pair, rolled), (rolled, pair))):
            for ref, value in ((lw, jnp.where(left, a, 0.0)), (rw, jnp.where(left, 0.0, b))):
                high, low = split(value)
                ref[2 * q + h, :, 0:128] = high
                ref[2 * q + h, :, 128:256] = low
        return carry

    def col_side(b, carry):
        off = pl.multiple_of(b * K, K)
        high, low = split(turned[pl.ds(off, K), :])
        first = jnp.clip(cols[b] - (leaf - REACH) * nodes, 0, last)
        second = jnp.clip(cols[b + 128] - (leaf - REACH) * nodes, 0, last)
        weights = jnp.concatenate([lw[first], rw[second]], axis=0)
        both = dot16(jnp.concatenate([high, low], axis=0), weights)
        turned[pl.ds(off, K), :] = both[:K, :128] + both[K:, :128] + both[:K, 128:]
        return carry

    def run(body, first, past, unroll):
        lax.fori_loop(first, past, body, 0, unroll=unroll)

    pairs = (2 * REACH + 1) * half
    window = []

    def send_window(slot, s, first, count):
        part = pl.ds(first, count)
        copy = send(win.at[REACH, part], win.at[REACH - s, part], ws.at[slot], wr.at[slot], (near(s), dom))
        window.append((copy, REACH - s, first, count))

    sends = [
        [(2, 0, half), (-2, 0, half)],
        [(1, 0, half), (-1, 0, half), (3, 0, half // 2), (-3, 0, half // 2)],
        [(3, half // 2, half // 2), (-3, half // 2, half // 2)],
    ]

    def send_windows(step):
        for what in sends[step]:
            send_window(len(window), *what)

    def prepare():
        for load in index_loads:
            load.wait()
        for arrival in gather:
            arrival.wait_recv()
        send_windows(0)
        run(expand_rows, 0, half, 2)

    def widen(first, past):
        for copy, _, _, _ in window[first:past]:
            copy.wait_recv()
        for _, s, begin, count in window[first:past]:
            run(expand_cols, s * half + begin, s * half + begin + count, 4)

    queues = {"turn": iter(range(K)), "row": iter(range(128)), "col": iter(range(128))}
    bodies = {"turn": turn, "row": row_side, "col": col_side}

    def hook(kind, total):
        def emit(point):
            points = K // 2
            for _ in range(total * (point + 1) // points - total * point // points):
                n = next(queues[kind], None)
                if n is not None:
                    bodies[kind](n, 0)
        return emit if total else None

    def chunk(kind, count, unroll):
        taken = list(itertools.islice(queues[kind], count))
        run(bodies[kind], taken[0], taken[-1] + 1, unroll)

    def fill(stage):
        if stage == 0:
            chunk("turn", TURN_FILL, 4)
            prepare()
        if stage == stages - 3:
            if stage:
                send_windows(1)
                chunk("row", ROW_FILL, 8)
            run(expand_cols, REACH * half, REACH * half + half, 4)
        elif stage == stages - 2:
            if stages < 4:
                send_windows(1)
            send_windows(2)
            chunk("row", None, 8)
            widen(0, 2)
        elif stage == stages - 1:
            widen(2, len(window))
            chunk("col", COL_FILL, 8)

    hooks = {0: ("row", ROW_HOOK, ROW_HOOK), stages - 3: ("row", ROW_HOOK, ROW_HOOK), stages - 1: ("col", COL_HOOK, 128 - COL_FILL - COL_HOOK)}

    child_copy.wait()
    stacked = [child[n] for n in range(per)]
    current = factor([dot(x, x, NT) for x in stacked])
    for m in range(own):
        tall = jnp.concatenate([current[2 * m][:, :K], current[2 * m + 1][:, :K]], axis=0)
        win[REACH, own * dom + m] = tall.T
    pl.semaphore_wait(barrier, len(greeted))
    mine = win.at[REACH, pl.ds(own * dom, own)]
    gather = spread(mine, gs, gr)

    for load in loads:
        load.wait()
    for n in range(3 * stages + 3):
        pair = par[n]
        par[n] = jnp.concatenate([pair[:, :K], pltpu.roll(pair, K, 1)[:, :K]], axis=0).T

    def product(packed, n):
        wide = jnp.concatenate([jnp.where(left, packed, 0.0), jnp.where(left, 0.0, packed)], axis=0)
        return dot(par[n], wide, NT)

    xa = [product(jnp.where(left, current[2 * s], pltpu.roll(current[2 * s + 1], K, 1)), s) for s in range(own)]
    below = current
    coup_copy.wait()
    current = factor([dot(x, x, NT) for x in xa], hook("turn", (K - TURN_FILL) // 2))
    x = product(jnp.where(left, current[0], pltpu.roll(current[1], K, 1)), own)
    for n in range(per):
        bottom_out[n] = dot(inverse(below[n]), stacked[n], NN)
    stores = [pltpu.make_async_copy(bottom_out, bottom_hbm, out_sem.at[0])]
    for s in range(own):
        local_out[own * dom + s] = dot(inverse(current[s]), xa[s], NN)
    (factored,) = factor([dot(x, x, NT)], hook("turn", (K - TURN_FILL) // 2))
    stores[0].start()
    arrivals = spread(local_out.at[pl.ds(own * dom, own)], bs, br)

    top_out[0] = jnp.zeros((K, 128), F32)

    def keep_bases(stage, lowers, xs, top, x):
        if stage == 0:
            for r, (lower, value) in enumerate(zip(lowers + [top], xs + [x])):
                local_out[half + doms + r] = dot(inverse(lower), value, NN)
            return
        first, second, middle = bases[stage - 1]
        at_first, at_middle = first == leaf, middle == leaf
        lower = jnp.where(at_middle, top, jnp.where(at_first, lowers[0], lowers[1]))
        value = jnp.where(at_middle, x, jnp.where(at_first, xs[0], xs[1]))
        found = at_first | at_middle | (second == leaf)
        top_out[0] = jnp.where(found, dot(inverse(lower), value, NN), top_out[0])

    pending = None
    for stage in range(stages):
        spot, others = groups[stage]
        xr[stage, spot] = jnp.where(lax.rem(spot, 2) == 0, factored, pltpu.roll(factored, K, 1))
        view = xr.at[stage, spot]
        copies = [send(view, view, es.at[stage, k], er.at[stage, k], others[k]) for k in range(3)]
        if stage == 0:
            local_out[half + dom] = dot(inverse(factored), x, NN)
            arrivals += spread(local_out.at[pl.ds(half + dom, 1)], cs, cr)
        else:
            keep_bases(*pending)
        fill(stage)
        for copy in copies:
            copy.wait_recv()
        kind, low, high = hooks.get(stage, ("row", 0, 0))
        xs = [product(jnp.where(left, xr[stage, 2 * s], xr[stage, 2 * s + 1]), 3 * stage + 3 + s) for s in range(2)]
        lowers = factor([dot(v, v, NT) for v in xs], hook(kind, low))
        if stage == stages - 1:
            ready = pl.ds(0, (COL_FILL + COL_HOOK) * K)
            stores.append(pltpu.make_async_copy(turned.at[ready], turned_hbm.at[ready], out_sem.at[1]))
            stores[-1].start()
            for copy in arrivals:
                copy.wait_recv()
            stores.append(pltpu.make_async_copy(local_out, local_hbm, out_sem.at[2]))
            stores[-1].start()
        x = product(jnp.where(left, lowers[0], pltpu.roll(lowers[1], K, 1)), 3 * stage + 5)
        (factored,) = factor([dot(x, x, NT)], hook(kind, high))
        pending = (stage, lowers, xs, factored, x)
    if COL_FILL + COL_HOOK < 128:
        ready = pl.ds((COL_FILL + COL_HOOK) * K, (128 - COL_FILL - COL_HOOK) * K)
        stores.append(pltpu.make_async_copy(turned.at[ready], turned_hbm.at[ready], out_sem.at[5]))
        stores[-1].start()
    root_out[...] = factored[:, :K]
    stores.append(pltpu.make_async_copy(root_out, root_hbm, out_sem.at[3]))
    stores[-1].start()
    keep_bases(*pending)
    stores.append(pltpu.make_async_copy(top_out, top_hbm, out_sem.at[4]))
    stores[-1].start()

    for copy in started:
        copy.wait_send()
    for copy in stores:
        copy.wait()


def finish(bottom, local, top, root, turned, bottom_out, local_out, top_out, root_out, proj_out,
           bottom_in, local_in, top_in, root_in, parts_in, ct, load_sem, part_sem, store_sem, out_sem):
    parts, _, deep, _ = parts_in.shape
    part_loads = []
    for part in range(parts):
        copy = pltpu.make_async_copy(turned.at[:, pl.ds(deep * part, deep)], parts_in.at[part], part_sem.at[part])
        copy.start()
        part_loads.append(copy)
    small = ((bottom, bottom_in, bottom_out), (local, local_in, local_out), (top, top_in, top_out), (root, root_in, root_out))
    loads = [pltpu.make_async_copy(src, mid, load_sem.at[n]) for n, (src, mid, _) in enumerate(small)]
    stores = [pltpu.make_async_copy(mid, dst, store_sem.at[n]) for n, (_, mid, dst) in enumerate(small)]
    for load in loads:
        load.start()
    for part in range(parts):
        part_loads[part].wait()
        for r in range(deep):
            slab = parts_in[part, :, r, :].T
            ct[deep * part + r, :, 0:128] = slab[:K]
            ct[deep * part + r, :, 128:256] = slab[K:]
        span = pl.ds(deep * part, deep)
        copy = pltpu.make_async_copy(ct.at[span], proj_out.at[span], out_sem.at[part])
        copy.start()
        stores.append(copy)
        if part == 0:
            for load, store in zip(loads, stores):
                load.wait()
                store.start()
    for copy in stores:
        copy.wait()


def on_device(doms, leaves, child_terms, transfer, top_transfer, coupling, block_row, block_col):
    per = child_terms.shape[0]
    nodes = per * doms
    top_levels = leaves.bit_length() - 1
    stages = (top_levels + doms.bit_length() - 1) // 2
    hbm = pl.BlockSpec(memory_space=pltpu.HBM)
    dma = pltpu.SemaphoreType.DMA
    sides = 2 * REACH
    small_shapes = ((per, K, 2 * K), (nodes - 1, K, 2 * K), (1, K, 2 * K), (K, K))
    small = tuple(jax.ShapeDtypeStruct(shape, F32) for shape in small_shapes)
    small_scratch = [pltpu.VMEM(shape, F32) for shape in small_shapes]
    *ready, turned = pl.pallas_call(
        functools.partial(kernel, doms, leaves),
        out_shape=small + (jax.ShapeDtypeStruct((128 * K, 128), F32),),
        in_specs=[hbm] * 6,
        out_specs=(hbm,) * 5,
        scratch_shapes=small_scratch + [
            pltpu.VMEM((128 * K, 128), F32),
            pltpu.VMEM((per, K, 128), F32),
            pltpu.SMEM((256,), jnp.int32),
            pltpu.SMEM((256,), jnp.int32),
            pltpu.VMEM((sides + 1, nodes // 2, K, 128), F32),
            pltpu.VMEM((K, K, 256), F32),
            pltpu.VMEM((3 * stages + 3, K, 128), F32),
            pltpu.VMEM((nodes, K, 256), BF),
            pltpu.VMEM(((sides + 1) * nodes, K, 256), BF),
            pltpu.VMEM(((sides + 1) * nodes, K, 256), BF),
            pltpu.VMEM((stages, 4, K, 128), F32),
            dma((3 * stages + 4,)),
            dma((6,)),
            dma((doms - 1,)), dma((doms - 1,)),
            dma((8,)), dma((8,)),
            dma((doms - 1,)), dma((doms - 1,)),
            dma((doms - 1,)), dma((doms - 1,)),
            dma((stages, 3)), dma((stages, 3)),
        ],
        compiler_params=pltpu.CompilerParams(
            collective_id=0, has_side_effects=True, vmem_limit_bytes=60 * 2**20),
    )(child_terms, transfer, top_transfer, jnp.transpose(coupling, (1, 2, 0)), block_row, block_col)
    bottom, local, top, root, projected = pl.pallas_call(
        finish,
        out_shape=small + (jax.ShapeDtypeStruct((K, K, 256), F32),),
        in_specs=[hbm] * 5,
        out_specs=(hbm,) * 5,
        scratch_shapes=small_scratch + [
            pltpu.VMEM((4, 128, K // 4, 128), F32), pltpu.VMEM((K, K, 256), F32),
            dma((4,)), dma((4,)), dma((4,)), dma((4,)),
        ],
        compiler_params=pltpu.CompilerParams(vmem_limit_bytes=60 * 2**20),
    )(*ready, turned.reshape(128, K, 128))
    return bottom, local, top, root, jnp.transpose(projected, (2, 0, 1))


def solution(mesh):
    split_all = P(("leaf", "dom"), None, None)
    placed = (split_all, P("leaf", None, None), P(), split_all, P(("leaf", "dom")), P(("leaf", "dom")))
    return jax.shard_map(
        functools.partial(on_device, mesh.shape["dom"], mesh.shape["leaf"]),
        mesh=mesh,
        in_specs=placed,
        out_specs=(split_all, P("leaf", None, None), P("leaf", None, None), P(), split_all),
        check_vma=False,
    )
```
